512 devices in a mesh: gx: 64 (over y, z_lo, core), gy: 8 (over x, z_hi).
Axes of the slice: x: 4, y: 8, z: 8 (z_hi: 2, z_lo: 4; z = z_hi * 4 + z_lo), core: 2. Of those that a mesh axis runs over, the one named last changes fastest.
Arguments:
- populations: float32 [27, 128, 32, 1024], P(None, 'gx', None, 'gy'), may hold values from 0.002 to 0.45, as said below
- fluid_mask: int32 [128, 32, 1024], P('gx', None, 'gy'), may hold values 0 or 1
Outputs:
- evolved: float32 [27, 128, 32, 1024], P(None, 'gx', None, 'gy')
The draws below stay inside these ranges and needn't reach their ends.
Inputs may be any that keep to these rules, and one draw needn't show every extreme that they name: `populations`: every population lies between 0.5 and 1.5 times its lattice weight, the weight being the product over the three components of 2/3 for 0 and 1/6 for -1 or 1.
All inputs are finite; a program needn't handle non-finite values. No bound on the sum of `fluid_mask` on one device may be relied on, other than what follows from the above.
Results may differ from the reference program's by a relative error of at most 0.0001.
Values sent between devices are 32-bit elements; how exact they have to be, the bound alone decides.
A program may use at most 64 MiB of HBM per device.

```python
import jax
import jax.numpy as jnp
from jax import lax

SLAB = 32
STEPS = 3
NX = 128
NY = 1024


def draw_populations(key, part):
    key = jax.random.fold_in(key, 11)
    base = jnp.array([1.0 / 6.0, 2.0 / 3.0, 1.0 / 6.0], jnp.float32)
    weights = (base[:, None, None] * base[None, :, None] * base[None, None, :]).reshape(27, 1, 1, 1)
    factor = jax.random.uniform(key, (27, NX, SLAB, NY), jnp.float32, 0.5, 1.5)
    return weights * factor


def with_ends(values, rng, least, largest):
    longest = values.shape.index(max(values.shape))
    spots = []
    for shift in (0, 1):
        where = [jax.random.randint(jax.random.fold_in(rng, axis), (), 0, length) for axis, length in enumerate(values.shape)]
        where[longest] = (where[longest] + shift) % values.shape[longest]
        spots.append(tuple(where))
    return values.at[spots[0]].set(least).at[spots[1]].set(largest)


def setup_inputs(seed: int = 0) -> dict:
    splits = jax.random.split(jax.random.key(seed), 3)
    populations = draw_populations(jax.random.fold_in(splits[2], 71), 0)
    fluid_mask = with_ends((jax.random.randint(splits[1], (NX, SLAB, NY), 0, 5) < 1).astype(jnp.int32), jax.random.fold_in(splits[1], 1), 0, 1)
    return {"populations": populations, "fluid_mask": fluid_mask}


shear_rate = 1.6
body_force = 0.002


def forward_triple(minus, rest, plus, speed):
    total = minus + rest + plus
    first = plus - minus
    second = plus + minus
    return (total, first - speed * total, second - 2.0 * speed * first + speed * speed * total)


def inverse_triple(zeroth, first, second, speed):
    raw_one = first + speed * zeroth
    raw_two = second + 2.0 * speed * first + speed * speed * zeroth
    return ((raw_two - raw_one) * 0.5, zeroth - raw_two, (raw_two + raw_one) * 0.5)


def collide(pops):
    density = jnp.sum(pops, axis=(0, 1, 2))
    speed_x = (jnp.sum(pops[2] - pops[0], axis=(0, 1)) + 0.5 * body_force) / density
    speed_y = jnp.sum(pops[:, 2] - pops[:, 0], axis=(0, 1)) / density
    speed_z = jnp.sum(pops[:, :, 2] - pops[:, :, 0], axis=(0, 1)) / density
    moments = jnp.stack(forward_triple(pops[0], pops[1], pops[2], speed_x), axis=0)
    moments = jnp.stack(forward_triple(moments[:, 0], moments[:, 1], moments[:, 2], speed_y), axis=1)
    moments = jnp.stack(forward_triple(moments[:, :, 0], moments[:, :, 1], moments[:, :, 2], speed_z), axis=2)
    keep = 1.0 - shear_rate
    trace = moments[2, 0, 0] + moments[0, 2, 0] + moments[0, 0, 2]
    s200 = keep * (moments[2, 0, 0] - trace / 3.0) + density / 3.0
    s020 = keep * (moments[0, 2, 0] - trace / 3.0) + density / 3.0
    s002 = keep * (moments[0, 0, 2] - trace / 3.0) + density / 3.0
    s110 = keep * moments[1, 1, 0]
    s101 = keep * moments[1, 0, 1]
    s011 = keep * moments[0, 1, 1]
    entries = {
        (0, 0, 0): density,
        (1, 0, 0): -moments[1, 0, 0],
        (0, 1, 0): -moments[0, 1, 0],
        (0, 0, 1): -moments[0, 0, 1],
        (2, 0, 0): s200, (0, 2, 0): s020, (0, 0, 2): s002,
        (1, 1, 0): s110, (1, 0, 1): s101, (0, 1, 1): s011,
        (2, 2, 0): (s200 * s020 + 2.0 * s110 * s110) / density,
        (2, 0, 2): (s200 * s002 + 2.0 * s101 * s101) / density,
        (0, 2, 2): (s020 * s002 + 2.0 * s011 * s011) / density,
        (2, 1, 1): (s200 * s011 + 2.0 * s110 * s101) / density,
        (1, 2, 1): (s020 * s101 + 2.0 * s110 * s011) / density,
        (1, 1, 2): (s002 * s110 + 2.0 * s101 * s011) / density,
        (2, 2, 2): (s200 * s020 * s002 + 2.0 * s110 * s110 * s002 + 2.0 * s101 * s101 * s020
                    + 2.0 * s011 * s011 * s200 + 8.0 * s110 * s101 * s011) / (density * density),
    }
    nothing = jnp.zeros_like(density)
    post = jnp.stack([jnp.stack([jnp.stack([entries.get((along_x, along_y, along_z), nothing)
                                            for along_z in range(3)]) for along_y in range(3)])
                      for along_x in range(3)])
    back = jnp.stack(inverse_triple(post[:, :, 0], post[:, :, 1], post[:, :, 2], speed_z), axis=2)
    back = jnp.stack(inverse_triple(back[:, 0], back[:, 1], back[:, 2], speed_y), axis=1)
    back = jnp.stack(inverse_triple(back[0], back[1], back[2], speed_x), axis=0)
    return back


def relax(pops, fluid):
    return jnp.where(fluid, collide(pops), pops[::-1, ::-1, ::-1])


def reference(populations, fluid_mask):
    state = jnp.transpose(populations, (1, 0, 2, 3))
    fluid = fluid_mask == 1

    def relax_sheet(operands):
        sheet, wet = operands
        pops = sheet.reshape(3, 3, 3, sheet.shape[1], sheet.shape[2])
        return relax(pops, wet).reshape(27, sheet.shape[1], sheet.shape[2])

    for step_index in range(STEPS):
        post = lax.map(relax_sheet, (state, fluid))
        moved = []
        for index in range(27):
            along_x = index // 9
            along_y = (index // 3) % 3
            along_z = index % 3
            moved.append(jnp.roll(post[:, index], (along_x - 1, along_z - 1, along_y - 1), axis=(0, 1, 2)))
        state = jnp.stack(moved, axis=1)
    return jnp.transpose(state, (1, 0, 2, 3))
```

```python
import jax
import jax.numpy as jnp
from jax import lax
from jax.experimental import pallas as pl
from jax.experimental.pallas import tpu as pltpu
from jax.sharding import PartitionSpec as P

STEPS = 3
MESH = pl.DeviceIdType.MESH

shear_rate = 1.6
body_force = 0.002
keep = 1.0 - shear_rate
third = 1.0 / 3.0

PAD = 8
NINE = 9


def inverse_triple(zeroth, first, second, speed):
    if zeroth is None:
        raw_one = first
        raw_two = 2.0 * speed * first
        rest = -raw_two
    else:
        if first is None:
            raw_one = speed * zeroth
            raw_two = second + speed * raw_one
        else:
            raw_one = first + speed * zeroth
            raw_two = speed * (first + raw_one)
            if second is not None:
                raw_two = second + raw_two
        rest = zeroth - raw_two
    plus = 0.5 * (raw_two + raw_one)
    return plus - raw_one, rest, plus


def collide(f):
    g = [[[f[9 * a + 3 * b + c] for c in range(3)] for b in range(3)] for a in range(3)]
    even = [[g[2][b][c] + g[0][b][c] for c in range(3)] for b in range(3)]
    diff = [[g[2][b][c] - g[0][b][c] for c in range(3)] for b in range(3)]
    total = [[even[b][c] + g[1][b][c] for c in range(3)] for b in range(3)]
    t_even = [total[2][c] + total[0][c] for c in range(3)]
    t_diff = [total[2][c] - total[0][c] for c in range(3)]
    t_total = [t_even[c] + total[1][c] for c in range(3)]
    d_total = [diff[2][c] + diff[0][c] + diff[1][c] for c in range(3)]
    d_diff = [diff[2][c] - diff[0][c] for c in range(3)]
    e_total = [even[2][c] + even[0][c] + even[1][c] for c in range(3)]
    m002 = t_total[2] + t_total[0]
    jz = t_total[2] - t_total[0]
    rho = m002 + t_total[1]
    jy = t_diff[0] + t_diff[1] + t_diff[2]
    m011 = t_diff[2] - t_diff[0]
    m020 = t_even[0] + t_even[1] + t_even[2]
    jx = d_total[0] + d_total[1] + d_total[2]
    m101 = d_total[2] - d_total[0]
    m110 = d_diff[0] + d_diff[1] + d_diff[2]
    m200 = e_total[0] + e_total[1] + e_total[2]
    r = 1.0 / rho
    ux = (jx + 0.5 * body_force) * r
    uy = jy * r
    uz = jz * r
    s100 = ux * rho - jx
    s010 = uy * rho - jy
    s001 = uz * rho - jz
    k200 = m200 - ux * (jx - s100)
    k020 = m020 - uy * (jy - s010)
    k002 = m002 - uz * (jz - s001)
    k110 = m110 - ux * jy + uy * s100
    k101 = m101 - ux * jz + uz * s100
    k011 = m011 - uy * jz + uz * s010
    base = third * rho - (keep * third) * (k200 + k020 + k002)
    s200 = keep * k200 + base
    s020 = keep * k020 + base
    s002 = keep * k002 + base
    s110 = keep * k110
    s101 = keep * k101
    s011 = keep * k011
    d110 = 2.0 * s110
    d101 = 2.0 * s101
    d011 = 2.0 * s011
    q110 = d110 * s110
    q101 = d101 * s101
    q011 = d011 * s011
    p220 = s200 * s020 + q110
    s220 = p220 * r
    s202 = (s200 * s002 + q101) * r
    s022 = (s020 * s002 + q011) * r
    s211 = (s200 * s011 + d110 * s101) * r
    s121 = (s020 * s101 + d110 * s011) * r
    s112 = (s002 * s110 + d101 * s011) * r
    s222 = (p220 * s002 + q101 * s020 + q011 * s200 + 2.0 * d110 * s101 * d011) * (r * r)
    along_z = [[None] * 3 for _ in range(3)]
    along_z[0][0] = inverse_triple(rho, s001, s002, uz)
    along_z[1][0] = inverse_triple(s100, s101, None, uz)
    along_z[0][1] = inverse_triple(s010, s011, None, uz)
    along_z[2][0] = inverse_triple(s200, None, s202, uz)
    along_z[0][2] = inverse_triple(s020, None, s022, uz)
    along_z[1][1] = inverse_triple(s110, None, s112, uz)
    along_z[2][1] = inverse_triple(None, s211, None, uz)
    along_z[1][2] = inverse_triple(None, s121, None, uz)
    along_z[2][2] = inverse_triple(s220, None, s222, uz)
    out = [None] * 27
    for c in range(3):
        along_y = [
            inverse_triple(along_z[a][0][c], along_z[a][1][c], along_z[a][2][c], uy)
            for a in range(3)
        ]
        for b in range(3):
            triple = inverse_triple(along_y[0][b], along_y[1][b], along_y[2][b], ux)
            for a in range(3):
                out[9 * a + 3 * b + c] = triple[a]
    return out


def kernel(count_x, count_y, f_hbm, m_hbm, o_hbm, f, mask, post, edge, near, halo, out,
           in_sem, out_sem, x_send, x_recv, y_send, y_recv):
    gx, gy = lax.axis_index("gx"), lax.axis_index("gy")
    core = lax.rem(gx, 2)
    depth = mask.shape[1]
    tiles = depth // 8

    def device(dx, dy):
        return (lax.rem(gx + dx + count_x, count_x), lax.rem(gy + dy + count_y, count_y))

    outer, inner = core, 1 - core
    loads = []
    for k, p in enumerate((outer, inner)):
        loads.append(
            (
                pltpu.make_async_copy(f_hbm.at[:, p], f.at[:, p], in_sem.at[2 * k]),
                pltpu.make_async_copy(m_hbm.at[p], mask.at[p], in_sem.at[2 * k + 1]),
            )
        )
        for copy in loads[-1]:
            copy.start()

    barrier = pltpu.get_barrier_semaphore()
    for dx in (-1, 0, 1):
        for dy in (-1, 0, 1):
            if dx or dy:
                pl.semaphore_signal(barrier, inc=1, device_id=device(dx, dy), device_id_type=MESH)

    lane = lax.broadcasted_iota(jnp.int32, (8, 128), 1)

    def x_copy(s, up):
        lo = 18 if up else 0
        here, there = (2, 0) if up else (1, 3)
        return pltpu.make_async_remote_copy(
            src_ref=post.at[s, pl.ds(lo, NINE), here, pl.ds(PAD, depth)],
            dst_ref=post.at[s, pl.ds(lo, NINE), there, pl.ds(PAD, depth)],
            send_sem=x_send.at[s, up],
            recv_sem=x_recv.at[s, up],
            device_id=device(1 if up else -1, 0),
            device_id_type=MESH,
        )

    def y_copy(s, up, dx):
        return pltpu.make_async_remote_copy(
            src_ref=edge.at[s, up],
            dst_ref=near.at[s, up, 1 - dx],
            send_sem=y_send.at[s, up, dx + 1],
            recv_sem=y_recv.at[s, up, 1 - dx],
            device_id=device(dx, 1 if up else -1),
            device_id_type=MESH,
        )

    def streamed(s, p, row):
        sides = [None, None]
        for up in (0, 1):
            sides[up] = [
                pltpu.roll(
                    halo[up, pl.ds(PAD + row - cz, 8), :], lax.rem(128 - NINE * p, 128), axis=1
                )
                for cz in (-1, 0, 1)
            ]
        pops = []
        for index in range(27):
            cx, cy, cz = index // 9 - 1, index // 3 % 3 - 1, index % 3 - 1
            value = post[s, index, p + 1 - cx, pl.ds(PAD + row - cz, 8), :]
            if cy:
                up = 1 if cy > 0 else 0
                place = (1 - cx) * NINE + 3 * (cx + 1) + cz + 1
                end = 0 if up else 127
                value = jnp.where(
                    lane == end,
                    pltpu.roll(sides[up][cz + 1], (end - place) % 128, axis=1),
                    pltpu.roll(value, 1 if up else 127, axis=1),
                )
            pops.append(value)
        return pops

    def relax(s, p, j):
        row = pl.multiple_of(8 * j, 8)
        if s == 0:
            pops = [f[index, p, pl.ds(row, 8), :] for index in range(27)]
        else:
            pops = streamed(s - 1, p, row)
        fluid = mask[p, pl.ds(row, 8), :] == 1
        after = collide(pops)
        after = [jnp.where(fluid, after[index], pops[26 - index]) for index in range(27)]
        again = jnp.where(j == 0, PAD + depth, jnp.where(j == tiles - 1, 0, PAD + row))
        again = pl.multiple_of(again, 8)
        for index in range(27):
            post[s, index, p + 1, pl.ds(PAD + row, 8), :] = after[index]
            post[s, index, p + 1, pl.ds(again, 8), :] = after[index]
        for up in (0, 1):
            packed = jnp.zeros((8, 128), jnp.float32)
            for k in range(NINE):
                index = 9 * (k // 3) + 6 * up + k % 3
                start = 127 if up else 0
                packed = jnp.where(
                    lane == k, pltpu.roll(after[index], (k - start) % 128, axis=1), packed
                )
            edge[s, up] = edge[s, up] + pltpu.roll(packed, NINE * (2 * j + p), axis=1)

    def sweep(s, p):
        def body(j, carry):
            relax(s, p, j)
            return carry

        lax.fori_loop(0, tiles, body, 0)

    def send(s, up):
        x_copy(s, up).start()

    def receive(s):
        for up in (0, 1):
            for dx in (-1, 0, 1):
                y_copy(s, up, dx).wait_recv()
        for up in (0, 1):
            for j in range(tiles):
                base = 2 * NINE * j
                low = pltpu.roll(near[s, up, 0], (-base - NINE) % 128, axis=1)
                mid = pltpu.roll(near[s, up, 1], (NINE - base) % 128, axis=1)
                high = pltpu.roll(near[s, up, 2], (3 * NINE - base) % 128, axis=1)
                rows = jnp.where(lane < NINE, low, jnp.where(lane < 3 * NINE, mid, high))
                halo[up, PAD + 8 * j : PAD + 8 * j + 8, :] = rows
                if j == 0:
                    halo[up, PAD + depth : PAD + depth + 8, :] = rows
                if j == tiles - 1:
                    halo[up, 0:8, :] = rows
        for up in (0, 1):
            x_copy(s, up).wait_recv()
            there, lo = (0, 18) if up else (3, 0)
            for index in range(lo, lo + NINE):
                post[s, index, there, 0:8, :] = post[s, index, there, depth : depth + 8, :]
                post[s, index, there, PAD + depth : PAD + depth + 8, :] = post[
                    s, index, there, PAD : PAD + 8, :
                ]

    edge[...] = jnp.zeros_like(edge)
    for s in range(STEPS):
        if s:
            receive(s - 1)
        else:
            for copy in loads[0]:
                copy.wait()
        sweep(s, outer)
        if s == 0:
            pl.semaphore_wait(barrier, 8)

        @pl.when(core == 0)
        def _():
            send(s, 0)

        @pl.when(core == 1)
        def _():
            send(s, 1)

        if s == 0:
            for copy in loads[1]:
                copy.wait()
        sweep(s, inner)
        for up in (0, 1):
            for dx in (-1, 0, 1):
                y_copy(s, up, dx).start()

        @pl.when(core == 0)
        def _():
            send(s, 1)

        @pl.when(core == 1)
        def _():
            send(s, 0)

    receive(STEPS - 1)

    def finish(j, carry):
        row = pl.multiple_of(8 * j, 8)
        for p in (0, 1):
            for index, value in enumerate(streamed(STEPS - 1, p, row)):
                out[index, p, pl.ds(row, 8), :] = value
        return carry

    stores = []
    for j in range(tiles):
        finish(j, 0)
        copy = pltpu.make_async_copy(
            out.at[:, :, pl.ds(8 * j, 8)], o_hbm.at[:, :, pl.ds(8 * j, 8)], out_sem.at[j]
        )
        copy.start()
        stores.append(copy)
    for s in range(STEPS):
        for up in (0, 1):
            x_copy(s, up).wait_send()
            for dx in (-1, 0, 1):
                y_copy(s, up, dx).wait_send()
    for copy in stores:
        copy.wait()


def solution(mesh):
    count_x, count_y = mesh.shape["gx"], mesh.shape["gy"]

    def on_device(populations, fluid_mask):
        width_x, depth, width_y = fluid_mask.shape
        tall = depth + 2 * PAD

        def body(*refs):
            kernel(count_x, count_y, *refs)

        return pl.pallas_call(
            body,
            out_shape=jax.ShapeDtypeStruct(populations.shape, jnp.float32),
            in_specs=[pl.BlockSpec(memory_space=pl.ANY)] * 2,
            out_specs=pl.BlockSpec(memory_space=pl.ANY),
            scratch_shapes=[
                pltpu.VMEM(populations.shape, jnp.float32),
                pltpu.VMEM(fluid_mask.shape, jnp.int32),
                pltpu.VMEM((STEPS, 27, width_x + 2, tall, width_y), jnp.float32),
                pltpu.VMEM((STEPS, 2, 8, 128), jnp.float32),
                pltpu.VMEM((STEPS, 2, 3, 8, 128), jnp.float32),
                pltpu.VMEM((2, tall, 128), jnp.float32),
                pltpu.VMEM(populations.shape, jnp.float32),
                pltpu.SemaphoreType.DMA((4,)),
                pltpu.SemaphoreType.DMA((depth // 8,)),
                pltpu.SemaphoreType.DMA((STEPS, 2)),
                pltpu.SemaphoreType.DMA((STEPS, 2)),
                pltpu.SemaphoreType.DMA((STEPS, 2, 3)),
                pltpu.SemaphoreType.DMA((STEPS, 2, 3)),
            ],
            compiler_params=pltpu.CompilerParams(
                collective_id=0, has_side_effects=True, vmem_limit_bytes=40 * 2**20
            ),
            cost_estimate=pl.CostEstimate(
                flops=500 * STEPS * fluid_mask.size,
                bytes_accessed=8 * populations.size,
                transcendentals=0,
            ),
            name="lattice_steps",
        )(populations, fluid_mask)

    in_specs = (P(None, "gx", None, "gy"), P("gx", None, "gy"))
    out_specs = P(None, "gx", None, "gy")
    return jax.shard_map(
        on_device, mesh=mesh, in_specs=in_specs, out_specs=out_specs, check_vma=False
    )
```

```python
import jax
import jax.numpy as jnp
from jax import lax
from jax.experimental import pallas as pl
from jax.experimental.pallas import tpu as pltpu
from jax.sharding import PartitionSpec as P

STEPS = 3
MESH = pl.DeviceIdType.MESH

shear_rate = 1.6
body_force = 0.002
keep = 1.0 - shear_rate
third = 1.0 / 3.0

PAD = 8
NINE = 9
NEIGHBOURS = [(dx, dy) for dx in (-1, 0, 1) for dy in (-1, 0, 1) if dx or dy]

OWN = {1: [(3, (4, 5))], 0: [(-1, (2,)), (2, (4,))], -1: [(-2, (1, 2))]}
SENT = {
    1: {1: (0, (0, 1, 2), 0, (0, 1, 2)), 0: (2, (3, 4), -3, (0, 1)), -1: (3, (5,), -5, (0,))},
    0: {-1: (-3, (0, 1, 2), 4, (4, 5, 6)), 0: (0, (3, 4), 2, (5, 6)), 1: (2, (5,), 1, (6,))},
}
MASK = 27


def inverse_triple(zeroth, first, second, speed):
    if zeroth is None:
        raw_one = first
        raw_two = 2.0 * speed * first
        rest = -raw_two
    else:
        if first is None:
            raw_one = speed * zeroth
            raw_two = second + speed * raw_one
        else:
            raw_one = first + speed * zeroth
            raw_two = speed * (first + raw_one)
            if second is not None:
                raw_two = second + raw_two
        rest = zeroth - raw_two
    plus = 0.5 * (raw_two + raw_one)
    return plus - raw_one, rest, plus


def collide(f):
    g = [[[f[9 * a + 3 * b + c] for c in range(3)] for b in range(3)] for a in range(3)]
    even = [[g[2][b][c] + g[0][b][c] for c in range(3)] for b in range(3)]
    diff = [[g[2][b][c] - g[0][b][c] for c in range(3)] for b in range(3)]
    total = [[even[b][c] + g[1][b][c] for c in range(3)] for b in range(3)]
    t_even = [total[2][c] + total[0][c] for c in range(3)]
    t_diff = [total[2][c] - total[0][c] for c in range(3)]
    t_total = [t_even[c] + total[1][c] for c in range(3)]
    d_total = [diff[2][c] + diff[0][c] + diff[1][c] for c in range(3)]
    d_diff = [diff[2][c] - diff[0][c] for c in range(3)]
    e_total = [even[2][c] + even[0][c] + even[1][c] for c in range(3)]
    m002 = t_total[2] + t_total[0]
    jz = t_total[2] - t_total[0]
    rho = m002 + t_total[1]
    jy = t_diff[0] + t_diff[1] + t_diff[2]
    m011 = t_diff[2] - t_diff[0]
    m020 = t_even[0] + t_even[1] + t_even[2]
    jx = d_total[0] + d_total[1] + d_total[2]
    m101 = d_total[2] - d_total[0]
    m110 = d_diff[0] + d_diff[1] + d_diff[2]
    m200 = e_total[0] + e_total[1] + e_total[2]
    r = 1.0 / rho
    ux = (jx + 0.5 * body_force) * r
    uy = jy * r
    uz = jz * r
    s100 = ux * rho - jx
    s010 = uy * rho - jy
    s001 = uz * rho - jz
    k200 = m200 - ux * (jx - s100)
    k020 = m020 - uy * (jy - s010)
    k002 = m002 - uz * (jz - s001)
    k110 = m110 - ux * jy + uy * s100
    k101 = m101 - ux * jz + uz * s100
    k011 = m011 - uy * jz + uz * s010
    base = third * rho - (keep * third) * (k200 + k020 + k002)
    s200 = keep * k200 + base
    s020 = keep * k020 + base
    s002 = keep * k002 + base
    s110 = keep * k110
    s101 = keep * k101
    s011 = keep * k011
    d110 = 2.0 * s110
    d101 = 2.0 * s101
    d011 = 2.0 * s011
    q110 = d110 * s110
    q101 = d101 * s101
    q011 = d011 * s011
    p220 = s200 * s020 + q110
    s220 = p220 * r
    s202 = (s200 * s002 + q101) * r
    s022 = (s020 * s002 + q011) * r
    s211 = (s200 * s011 + d110 * s101) * r
    s121 = (s020 * s101 + d110 * s011) * r
    s112 = (s002 * s110 + d101 * s011) * r
    s222 = (p220 * s002 + q101 * s020 + q011 * s200 + 2.0 * d110 * s101 * d011) * (r * r)
    along_z = [[None] * 3 for _ in range(3)]
    along_z[0][0] = inverse_triple(rho, s001, s002, uz)
    along_z[1][0] = inverse_triple(s100, s101, None, uz)
    along_z[0][1] = inverse_triple(s010, s011, None, uz)
    along_z[2][0] = inverse_triple(s200, None, s202, uz)
    along_z[0][2] = inverse_triple(s020, None, s022, uz)
    along_z[1][1] = inverse_triple(s110, None, s112, uz)
    along_z[2][1] = inverse_triple(None, s211, None, uz)
    along_z[1][2] = inverse_triple(None, s121, None, uz)
    along_z[2][2] = inverse_triple(s220, None, s222, uz)
    out = [None] * 27
    for c in range(3):
        along_y = [
            inverse_triple(along_z[a][0][c], along_z[a][1][c], along_z[a][2][c], uy)
            for a in range(3)
        ]
        for b in range(3):
            triple = inverse_triple(along_y[0][b], along_y[1][b], along_y[2][b], ux)
            for a in range(3):
                out[9 * a + 3 * b + c] = triple[a]
    return out


def turn(value, shift):
    return pltpu.roll(value, shift % 128, axis=1) if shift % 128 else value


def number(cx, cy, cz):
    return 9 * (cx + 1) + 3 * (cy + 1) + cz + 1


def kernel(count_x, count_y, f_hbm, m_hbm, out, f, mask, post, rim, fringe, fringe_mask, halo,
           y_out, y_in, d_in, e_out, e_in,
           in_sem, x_send, x_recv, e_send, e_recv, y_send, y_recv):
    gx, gy = lax.axis_index("gx"), lax.axis_index("gy")
    depth = mask.shape[1]
    tiles = depth // 8

    def device(dx, dy):
        return (lax.rem(gx + dx + count_x, count_x), lax.rem(gy + dy + count_y, count_y))

    barrier = pltpu.get_barrier_semaphore()
    for dx, dy in NEIGHBOURS:
        pl.semaphore_signal(barrier, inc=1, device_id=device(dx, dy), device_id_type=MESH)
    loads = [
        pltpu.make_async_copy(f_hbm, f, in_sem.at[0]),
        pltpu.make_async_copy(m_hbm, mask, in_sem.at[1]),
    ]
    for copy in loads:
        copy.start()

    lane = lax.broadcasted_iota(jnp.int32, (8, 128), 1)
    line = lax.broadcasted_iota(jnp.int32, (8, 128), 0)
    column = lane % 8
    plane = (lane // 8) % 4

    def among(lanes, planes):
        low, high = lanes[0], lanes[-1]
        here = (column >= low) & (column <= high) if low < high else column == low
        one = plane == planes[0]
        for other in planes[1:]:
            one = one | (plane == other)
        return here & one

    def x_copy(s, up):
        lo = 18 if up else 0
        here, there = (2, 0) if up else (1, 3)
        return pltpu.make_async_remote_copy(
            src_ref=post.at[s, pl.ds(lo, NINE), here, pl.ds(PAD, depth)],
            dst_ref=post.at[s, pl.ds(lo, NINE), there, pl.ds(PAD, depth)],
            send_sem=x_send.at[s, up],
            recv_sem=x_recv.at[s, up],
            device_id=device(1 if up else -1, 0),
            device_id_type=MESH,
        )

    def e_copy(s, up):
        return pltpu.make_async_remote_copy(
            src_ref=e_out.at[s, up],
            dst_ref=e_in.at[s, up],
            send_sem=e_send.at[s, up],
            recv_sem=e_recv.at[s, up],
            device_id=device(1 if up else -1, 0),
            device_id_type=MESH,
        )

    def y_copy(up, dx):
        if dx:
            src, dst = y_out.at[up, pl.ds(3 if dx > 0 else 0, 2)], d_in.at[up, (1 - dx) // 2]
        else:
            src, dst = y_out.at[up], y_in.at[up]
        return pltpu.make_async_remote_copy(
            src_ref=src,
            dst_ref=dst,
            send_sem=y_send.at[up, dx + 1],
            recv_sem=y_recv.at[up, 1 - dx],
            device_id=device(dx, 1 if up else -1),
            device_id_type=MESH,
        )

    def relax(s):
        def body(j, carry):
            row = pl.multiple_of(8 * j, 8)
            again = jnp.where(j == 0, PAD + depth, jnp.where(j == tiles - 1, 0, PAD + row))
            again = pl.multiple_of(again, 8)
            for p in (0, 1):
                pops = [f[index, p, pl.ds(row, 8), :] for index in range(27)]
                fluid = mask[p, pl.ds(row, 8), :] == 1
                after = collide(pops)
                for index in range(27):
                    value = jnp.where(fluid, after[index], pops[26 - index])
                    post[s, index, p + 1, pl.ds(PAD + row, 8), :] = value
                    post[s, index, p + 1, pl.ds(again, 8), :] = value
            return carry

        lax.fori_loop(0, tiles, body, 0)

    def make_rim():
        def gather(tile):
            packed = None
            for j in range(tiles):
                for p in (0, 1):
                    start = 32 * j + 8 * (p + 1)
                    value = turn(tile(j, p), start - 125)
                    here = (lane >= start) & (lane < start + 8)
                    packed = value if packed is None else jnp.where(here, value, packed)
            return packed

        def body(third, carry):
            for k in range(3):
                index = 3 * third + k
                rim[index] = gather(lambda j, p: post[0, index, p + 1, PAD + 8 * j : PAD + 8 * j + 8, :])
            return carry

        lax.fori_loop(0, NINE, body, 0)
        rim[MASK] = gather(lambda j, p: mask[p, 8 * j : 8 * j + 8, :].astype(jnp.float32))

    def own_part(index, cy):
        value = None
        for shift, lanes in OWN[cy]:
            moved = turn(rim[index], shift)
            value = moved if value is None else jnp.where(among(lanes, (1, 2)), moved, value)
        return value

    def slot(t):
        return t // 2, 16 * (t % 2), (3, 0) if t % 2 else (1, 2)

    def make_messages():
        for up in (0, 1):
            packed = [jnp.zeros((8, 128), jnp.float32)] * 5
            for t in range(10):
                tile, extra, planes = slot(t)
                for cy in (-1, 0, 1):
                    if t == NINE and cy:
                        continue
                    index = MASK if t == NINE else number(t // 3 - 1, cy, t % 3 - 1)
                    shift, lanes, _, _ = SENT[up][cy]
                    value = turn(rim[index], shift + extra)
                    packed[tile] = jnp.where(among(lanes, planes), value, packed[tile])
            for tile in range(5):
                y_out[up, tile] = packed[tile]

    def from_side(ref, first, t, cy, up, across, planes, value):
        tile, extra, _ = slot(t)
        _, _, shift, lanes = SENT[up][cy]
        moved = turn(ref[tile - first], shift - extra + across)
        return jnp.where(among(lanes, planes), moved, value)

    def send_fringe(s):
        for up in (0, 1):
            for tile in range(3):
                packed = None
                for q in range(4 * tile, min(4 * tile + 4, NINE)):
                    value = turn(fringe[18 * up + q], 8 * (q % 4 - 1 - up))
                    packed = value if packed is None else jnp.where(plane == q % 4, value, packed)
                e_out[s, up, tile] = packed
            e_copy(s, up).start()

    def receive_fringe(s):
        for up in (0, 1):
            e_copy(s, up).wait_recv()
            there = 0 if up else 3
            for q in range(NINE):
                index = 18 * up + q
                moved = turn(e_in[s, up, q // 4], 8 * (there - q % 4))
                fringe[index] = jnp.where(plane == there, moved, fringe[index])

    def receive_sides():
        for up in (0, 1):
            for dx in (-1, 0, 1):
                y_copy(up, dx).wait_recv()
        for t in range(NINE):
            cx = t // 3 - 1
            for cy in (-1, 0, 1):
                index = number(cx, cy, t % 3 - 1)
                value = fringe[index]
                for up in (0, 1):
                    value = from_side(y_in.at[up], 0, t, cy, up, 0, (1, 2), value)
                    if cx:
                        near = d_in.at[up, 0 if cx > 0 else 1]
                        first, there = (3, 0) if cx > 0 else (0, 3)
                        value = from_side(near, first, t, cy, up, -16 * cx, (there,), value)
                fringe[index] = value
        value = own_part(MASK, 0)
        for up in (0, 1):
            value = from_side(y_in.at[up], 0, NINE, 0, up, 0, (1, 2), value)
        fringe_mask[...] = value

    def lay_out():
        by_cx = []
        for cx in (-1, 0, 1):
            value = None
            for cz in (-1, 0, 1):
                for cy in (1, -1):
                    target = 2 * (cz + 1) + (1 if cy > 0 else 0)
                    moved = turn(fringe[number(cx, cy, cz)], target - (2 if cy > 0 else 4))
                    value = moved if value is None else jnp.where(column == target, moved, value)
            by_cx.append(value)
        block = lane // 32
        for j in range(tiles):
            parts = [turn(by_cx[b], 32 * (b - j)) for b in range(3)]
            rows = jnp.where(block == 0, parts[0], jnp.where(block == 1, parts[1], parts[2]))
            halo[PAD + 8 * j : PAD + 8 * j + 8, :] = rows
            if j == 0:
                halo[PAD + depth : PAD + depth + 8, :] = rows
            if j == tiles - 1:
                halo[0:8, :] = rows

    def step_fringe():
        pops = []
        for index in range(27):
            cx, cz = index // 9 - 1, index % 3 - 1
            value = turn(fringe[index], 8 * cx)
            if cz:
                value = pltpu.roll(value, cz % 8, axis=0)
                value = jnp.where(line == (0 if cz > 0 else 7), turn(value, 32 * cz), value)
            pops.append(value)
        after = collide(pops)
        fluid = fringe_mask[...] == 1.0
        for index in range(27):
            value = jnp.where(fluid, after[index], pops[26 - index])
            fringe[index] = turn(value, index // 3 % 3 - 1)

    def ends(row, p, cx, cz):
        place = 32 * (cx + 1) + 8 * (p + 1 - cx) + 2 * (cz + 1) + 1
        return pltpu.roll(halo[pl.ds(PAD + row - cz, 8), :], (-place) % 128, axis=1)

    def place_own(s, to):
        def body(j, carry):
            row = pl.multiple_of(8 * j, 8)
            for p in (0, 1):
                for cx in (0, 2 * p - 1):
                    for cy in (-1, 0, 1):
                        for cz in (-1, 0, 1):
                            index = 9 * (cx + 1) + 3 * (cy + 1) + cz + 1
                            value = post[s, index, p + 1 - cx, pl.ds(PAD + row - cz, 8), :]
                            if cy:
                                value = pltpu.roll(value, cy % 128, axis=1)
                            to[index, p, pl.ds(row, 8), :] = value
            return carry

        lax.fori_loop(0, tiles, body, 0)

    def place_edges(to):
        def body(j, carry):
            row = pl.multiple_of(8 * j, 8)
            for p in (0, 1):
                for cx in (0, 2 * p - 1):
                    for cz in (-1, 0, 1):
                        both = ends(row, p, cx, cz)
                        for cy in (-1, 1):
                            index = 9 * (cx + 1) + 3 * (cy + 1) + cz + 1
                            value = to[index, p, pl.ds(row, 8), :]
                            end = 0 if cy > 0 else 127
                            to[index, p, pl.ds(row, 8), :] = jnp.where(lane == end, both, value)
            return carry

        lax.fori_loop(0, tiles, body, 0)

    def place_faces(s, to):
        for there, lo in ((0, 18), (3, 0)):
            for index in range(lo, lo + NINE):
                post[s, index, there, 0:8, :] = post[s, index, there, depth : depth + 8, :]
                post[s, index, there, PAD + depth : PAD + depth + 8, :] = post[
                    s, index, there, PAD : PAD + 8, :
                ]

        def body(j, carry):
            row = pl.multiple_of(8 * j, 8)
            for p in (0, 1):
                cx = 1 - 2 * p
                for cz in (-1, 0, 1):
                    both = ends(row, p, cx, cz)
                    for cy in (-1, 0, 1):
                        index = 9 * (cx + 1) + 3 * (cy + 1) + cz + 1
                        value = post[s, index, p + 1 - cx, pl.ds(PAD + row - cz, 8), :]
                        if cy:
                            value = pltpu.roll(value, cy % 128, axis=1)
                            end = 0 if cy > 0 else 127
                            value = jnp.where(lane == end, both, value)
                        to[index, p, pl.ds(row, 8), :] = value
            return carry

        lax.fori_loop(0, tiles, body, 0)

    for copy in loads:
        copy.wait()
    relax(0)
    make_rim()
    make_messages()
    for index in range(27):
        fringe[index] = own_part(index, index // 3 % 3 - 1)
    pl.semaphore_wait(barrier, len(NEIGHBOURS))
    for up in (0, 1):
        for dx in (0, -1, 1):
            y_copy(up, dx).start()
    send_fringe(0)
    for s in range(STEPS):
        last = s == STEPS - 1
        to = out if last else f
        for up in (0, 1):
            x_copy(s, up).start()
        place_own(s, to)
        receive_fringe(s)
        if s == 0:
            receive_sides()
        lay_out()
        if not last:
            step_fringe()
            send_fringe(s + 1)
        place_edges(to)
        for up in (0, 1):
            x_copy(s, up).wait_recv()
        place_faces(s, to)
        if not last:
            relax(s + 1)
    for up in (0, 1):
        for dx in (-1, 0, 1):
            y_copy(up, dx).wait_send()
        for s in range(STEPS):
            x_copy(s, up).wait_send()
            e_copy(s, up).wait_send()


def solution(mesh):
    count_x, count_y = mesh.shape["gx"], mesh.shape["gy"]

    def on_device(populations, fluid_mask):
        width_x, depth, width_y = fluid_mask.shape
        tall = depth + 2 * PAD

        def body(*refs):
            kernel(count_x, count_y, *refs)

        return pl.pallas_call(
            body,
            out_shape=pltpu.VMEM(populations.shape, jnp.float32),
            in_specs=[pl.BlockSpec(memory_space=pltpu.HBM)] * 2,
            out_specs=pl.BlockSpec(memory_space=pltpu.VMEM),
            scratch_shapes=[
                pltpu.VMEM(populations.shape, jnp.float32),
                pltpu.VMEM(fluid_mask.shape, jnp.int32),
                pltpu.VMEM((STEPS, 27, width_x + 2, tall, width_y), jnp.float32),
                pltpu.VMEM((MASK + 1, 8, 128), jnp.float32),
                pltpu.VMEM((27, 8, 128), jnp.float32),
                pltpu.VMEM((8, 128), jnp.float32),
                pltpu.VMEM((tall, 128), jnp.float32),
                pltpu.VMEM((2, 5, 8, 128), jnp.float32),
                pltpu.VMEM((2, 5, 8, 128), jnp.float32),
                pltpu.VMEM((2, 2, 2, 8, 128), jnp.float32),
                pltpu.VMEM((STEPS, 2, 3, 8, 128), jnp.float32),
                pltpu.VMEM((STEPS, 2, 3, 8, 128), jnp.float32),
                pltpu.SemaphoreType.DMA((2,)),
                pltpu.SemaphoreType.DMA((STEPS, 2)),
                pltpu.SemaphoreType.DMA((STEPS, 2)),
                pltpu.SemaphoreType.DMA((STEPS, 2)),
                pltpu.SemaphoreType.DMA((STEPS, 2)),
                pltpu.SemaphoreType.DMA((2, 3)),
                pltpu.SemaphoreType.DMA((2, 3)),
            ],
            compiler_params=pltpu.CompilerParams(
                collective_id=0, has_side_effects=True, vmem_limit_bytes=60 * 2**20
            ),
            cost_estimate=pl.CostEstimate(
                flops=500 * STEPS * fluid_mask.size,
                bytes_accessed=8 * populations.size,
                transcendentals=0,
            ),
            name="lattice_steps",
        )(populations, fluid_mask)

    in_specs = (P(None, "gx", None, "gy"), P("gx", None, "gy"))
    out_specs = P(None, "gx", None, "gy")
    return jax.shard_map(
        on_device, mesh=mesh, in_specs=in_specs, out_specs=out_specs, check_vma=False
    )
```

```python
import jax
import jax.numpy as jnp
from jax import lax
from jax.experimental import pallas as pl
from jax.experimental.pallas import tpu as pltpu
from jax.sharding import PartitionSpec as P

STEPS = 3
MESH = pl.DeviceIdType.MESH

shear_rate = 1.6
body_force = 0.002
keep = 1.0 - shear_rate
third = 1.0 / 3.0

PAD = 8
NINE = 9
NEIGHBOURS = [(dx, dy) for dx in (-1, 0, 1) for dy in (-1, 0, 1) if dx or dy]

OWN = {1: [(0, (3,)), (4, (4, 5, 6))], 0: [(-1, (2, 3)), (3, (4, 5))], -1: [(-2, (1, 2, 3)), (2, (4,))]}
SENT = {
    1: {1: (0, (0, 1, 2), 0, (0, 1, 2)), 0: (2, (3, 4), -3, (0, 1)), -1: (3, (5,), -5, (0,))},
    0: {-1: (-3, (0, 1, 2), 5, (5, 6, 7)), 0: (0, (3, 4), 3, (6, 7)), 1: (2, (5,), 2, (7,))},
}
MASK = 27


def inverse_triple(zeroth, first, second, speed):
    if zeroth is None:
        raw_one = first
        raw_two = 2.0 * speed * first
        rest = -raw_two
    else:
        if first is None:
            raw_one = speed * zeroth
            raw_two = second + speed * raw_one
        else:
            raw_one = first + speed * zeroth
            raw_two = speed * (first + raw_one)
            if second is not None:
                raw_two = second + raw_two
        rest = zeroth - raw_two
    plus = 0.5 * (raw_two + raw_one)
    return plus - raw_one, rest, plus


def collide(f):
    g = [[[f[9 * a + 3 * b + c] for c in range(3)] for b in range(3)] for a in range(3)]
    even = [[g[2][b][c] + g[0][b][c] for c in range(3)] for b in range(3)]
    diff = [[g[2][b][c] - g[0][b][c] for c in range(3)] for b in range(3)]
    total = [[even[b][c] + g[1][b][c] for c in range(3)] for b in range(3)]
    t_even = [total[2][c] + total[0][c] for c in range(3)]
    t_diff = [total[2][c] - total[0][c] for c in range(3)]
    t_total = [t_even[c] + total[1][c] for c in range(3)]
    d_total = [diff[2][c] + diff[0][c] + diff[1][c] for c in range(3)]
    d_diff = [diff[2][c] - diff[0][c] for c in range(3)]
    e_total = [even[2][c] + even[0][c] + even[1][c] for c in range(3)]
    m002 = t_total[2] + t_total[0]
    jz = t_total[2] - t_total[0]
    rho = m002 + t_total[1]
    jy = t_diff[0] + t_diff[1] + t_diff[2]
    m011 = t_diff[2] - t_diff[0]
    m020 = t_even[0] + t_even[1] + t_even[2]
    jx = d_total[0] + d_total[1] + d_total[2]
    m101 = d_total[2] - d_total[0]
    m110 = d_diff[0] + d_diff[1] + d_diff[2]
    m200 = e_total[0] + e_total[1] + e_total[2]
    r = 1.0 / rho
    ux = (jx + 0.5 * body_force) * r
    uy = jy * r
    uz = jz * r
    s100 = ux * rho - jx
    s010 = uy * rho - jy
    s001 = uz * rho - jz
    k200 = m200 - ux * (jx - s100)
    k020 = m020 - uy * (jy - s010)
    k002 = m002 - uz * (jz - s001)
    k110 = m110 - ux * jy + uy * s100
    k101 = m101 - ux * jz + uz * s100
    k011 = m011 - uy * jz + uz * s010
    base = third * rho - (keep * third) * (k200 + k020 + k002)
    s200 = keep * k200 + base
    s020 = keep * k020 + base
    s002 = keep * k002 + base
    s110 = keep * k110
    s101 = keep * k101
    s011 = keep * k011
    d110 = 2.0 * s110
    d101 = 2.0 * s101
    d011 = 2.0 * s011
    q110 = d110 * s110
    q101 = d101 * s101
    q011 = d011 * s011
    p220 = s200 * s020 + q110
    s220 = p220 * r
    s202 = (s200 * s002 + q101) * r
    s022 = (s020 * s002 + q011) * r
    s211 = (s200 * s011 + d110 * s101) * r
    s121 = (s020 * s101 + d110 * s011) * r
    s112 = (s002 * s110 + d101 * s011) * r
    s222 = (p220 * s002 + q101 * s020 + q011 * s200 + 2.0 * d110 * s101 * d011) * (r * r)
    along_z = [[None] * 3 for _ in range(3)]
    along_z[0][0] = inverse_triple(rho, s001, s002, uz)
    along_z[1][0] = inverse_triple(s100, s101, None, uz)
    along_z[0][1] = inverse_triple(s010, s011, None, uz)
    along_z[2][0] = inverse_triple(s200, None, s202, uz)
    along_z[0][2] = inverse_triple(s020, None, s022, uz)
    along_z[1][1] = inverse_triple(s110, None, s112, uz)
    along_z[2][1] = inverse_triple(None, s211, None, uz)
    along_z[1][2] = inverse_triple(None, s121, None, uz)
    along_z[2][2] = inverse_triple(s220, None, s222, uz)
    out = [None] * 27
    for c in range(3):
        along_y = [
            inverse_triple(along_z[a][0][c], along_z[a][1][c], along_z[a][2][c], uy)
            for a in range(3)
        ]
        for b in range(3):
            triple = inverse_triple(along_y[0][b], along_y[1][b], along_y[2][b], ux)
            for a in range(3):
                out[9 * a + 3 * b + c] = triple[a]
    return out


def turn(value, shift):
    return pltpu.roll(value, shift % 128, axis=1) if shift % 128 else value


def number(cx, cy, cz):
    return 9 * (cx + 1) + 3 * (cy + 1) + cz + 1


def kernel(count_x, count_y, f_hbm, m_hbm, out, f, mask, post, rim, fringe, fringe_mask, halo,
           y_out, y_in, d_in, e_out, e_in,
           in_sem, x_send, x_recv, e_send, e_recv, y_send, y_recv):
    gx, gy = lax.axis_index("gx"), lax.axis_index("gy")
    depth = post.shape[3] - 2 * PAD
    tiles = depth // 8

    def device(dx, dy):
        return (lax.rem(gx + dx + count_x, count_x), lax.rem(gy + dy + count_y, count_y))

    barrier = pltpu.get_barrier_semaphore()
    for dx, dy in NEIGHBOURS:
        pl.semaphore_signal(barrier, inc=1, device_id=device(dx, dy), device_id_type=MESH)
    loads = [
        pltpu.make_async_copy(f_hbm, f, in_sem.at[0]),
        pltpu.make_async_copy(m_hbm, mask.at[:, pl.ds(0, depth)], in_sem.at[1]),
    ]
    for copy in loads:
        copy.start()

    lane = lax.broadcasted_iota(jnp.int32, (8, 128), 1)
    line = lax.broadcasted_iota(jnp.int32, (8, 128), 0)
    column = lane % 8
    plane = (lane // 8) % 4

    def among(lanes, planes):
        low, high = lanes[0], lanes[-1]
        here = (column >= low) & (column <= high) if low < high else column == low
        one = plane == planes[0]
        for other in planes[1:]:
            one = one | (plane == other)
        return here & one

    def x_copy(s, up, j):
        rows = pl.ds(PAD + 8 * j, 8)
        lo = 18 if up else 0
        here, there = (2, 0) if up else (1, 3)
        return pltpu.make_async_remote_copy(
            src_ref=post.at[s, pl.ds(lo, NINE), here, rows],
            dst_ref=post.at[s, pl.ds(lo, NINE), there, rows],
            send_sem=x_send.at[s, up, j],
            recv_sem=x_recv.at[s, up, j],
            device_id=device(1 if up else -1, 0),
            device_id_type=MESH,
        )

    def e_copy(s, up):
        return pltpu.make_async_remote_copy(
            src_ref=e_out.at[s, up],
            dst_ref=e_in.at[s, up],
            send_sem=e_send.at[s, up],
            recv_sem=e_recv.at[s, up],
            device_id=device(1 if up else -1, 0),
            device_id_type=MESH,
        )

    def y_copy(up, dx):
        if dx:
            src, dst = y_out.at[up, pl.ds(3 if dx > 0 else 0, 2)], d_in.at[up, (1 - dx) // 2]
        else:
            src, dst = y_out.at[up], y_in.at[up]
        return pltpu.make_async_remote_copy(
            src_ref=src,
            dst_ref=dst,
            send_sem=y_send.at[up, dx + 1],
            recv_sem=y_recv.at[up, 1 - dx],
            device_id=device(dx, 1 if up else -1),
            device_id_type=MESH,
        )

    def shift_of(s):
        return 1 if s < STEPS - 1 else 1 - STEPS

    def streamed(s, p, cx, row):
        pops = {}
        for cz in (-1, 0, 1):
            for cy in (-1, 0, 1):
                value = post[s, number(cx, cy, cz), p + 1 - cx, pl.ds(PAD + row + shift_of(s) - cz, 8), :]
                if cy:
                    value = pltpu.roll(value, cy % 128, axis=1)
                pops[number(cx, cy, cz)] = value
            with_ends(s, row, p, cx, cz, pops)
        return pops

    def relax(s):
        def body(j, carry):
            row = pl.multiple_of(8 * j, 8)
            again = jnp.where(j == 0, PAD + depth, jnp.where(j == tiles - 1, 0, PAD + row))
            again = pl.multiple_of(again, 8)
            if s:

                @pl.when(j < tiles - 1)
                def _():
                    for up in (0, 1):
                        x_copy(s - 1, up, j + 1).wait_recv()

            for p in (0, 1):
                far = streamed(s - 1, p, 1 - 2 * p, row) if s else {}
                pops = [
                    far[index] if index in far else f[index, p, pl.ds(row, 8), :]
                    for index in range(27)
                ]
                fluid = mask[p, pl.ds(row + s, 8), :] == 1
                after = collide(pops)
                for index in range(27):
                    value = jnp.where(fluid, after[index], pops[26 - index])
                    post[s, index, p + 1, pl.ds(PAD + row, 8), :] = value
                    post[s, index, p + 1, pl.ds(again, 8), :] = value
            if s:
                for up in (0, 1):
                    x_copy(s, up, j).start()
            return carry

        if s:
            for up in (0, 1):
                x_copy(s - 1, up, 0).wait_recv()
            wrap_faces(s - 1, PAD, PAD + depth)
        lax.fori_loop(0, tiles, body, 0)

    def wrap_faces(s, start, end):
        for there, lo in ((0, 18), (3, 0)):
            for index in range(lo, lo + NINE):
                post[s, index, there, end : end + 8, :] = post[s, index, there, start : start + 8, :]

    def make_rim():
        def gather(tile):
            packed = None
            for j in range(tiles):
                for p in (0, 1):
                    start = 32 * j + 8 * (p + 1)
                    value = turn(tile(j, p), start - 125)
                    here = (lane >= start) & (lane < start + 8)
                    packed = value if packed is None else jnp.where(here, value, packed)
            return packed

        def body(third, carry):
            for k in range(3):
                index = 3 * third + k
                rim[index] = gather(lambda j, p: post[0, index, p + 1, PAD + 8 * j : PAD + 8 * j + 8, :])
            return carry

        lax.fori_loop(0, NINE, body, 0)
        rim[MASK] = gather(lambda j, p: mask[p, 8 * j : 8 * j + 8, :].astype(jnp.float32))

    def own_part(index, cy):
        value = None
        for shift, lanes in OWN[cy]:
            moved = turn(rim[index], shift)
            value = moved if value is None else jnp.where(among(lanes, (1, 2)), moved, value)
        return value

    def slot(t):
        return t // 2, 16 * (t % 2), (3, 0) if t % 2 else (1, 2)

    def make_messages():
        for up in (0, 1):
            packed = [jnp.zeros((8, 128), jnp.float32)] * 5
            for t in range(10):
                tile, extra, planes = slot(t)
                for cy in (-1, 0, 1):
                    if t == NINE and cy:
                        continue
                    index = MASK if t == NINE else number(t // 3 - 1, cy, t % 3 - 1)
                    shift, lanes, _, _ = SENT[up][cy]
                    value = turn(rim[index], shift + extra)
                    packed[tile] = jnp.where(among(lanes, planes), value, packed[tile])
            for tile in range(5):
                y_out[up, tile] = packed[tile]

    def from_side(ref, first, t, cy, up, across, planes, value):
        tile, extra, _ = slot(t)
        _, _, shift, lanes = SENT[up][cy]
        moved = turn(ref[tile - first], shift - extra + across)
        return jnp.where(among(lanes, planes), moved, value)

    def send_fringe(s):
        for up in (0, 1):
            for tile in range(3):
                packed = None
                for q in range(4 * tile, min(4 * tile + 4, NINE)):
                    value = turn(fringe[18 * up + q], 8 * (q % 4 - 1 - up))
                    packed = value if packed is None else jnp.where(plane == q % 4, value, packed)
                e_out[s, up, tile] = packed
            e_copy(s, up).start()

    def receive_fringe(s):
        for up in (0, 1):
            e_copy(s, up).wait_recv()
            there = 0 if up else 3
            for q in range(NINE):
                index = 18 * up + q
                moved = turn(e_in[s, up, q // 4], 8 * (there - q % 4))
                fringe[index] = jnp.where(plane == there, moved, fringe[index])

    def receive_sides():
        for up in (0, 1):
            for dx in (-1, 0, 1):
                y_copy(up, dx).wait_recv()
        for t in range(NINE):
            cx = t // 3 - 1
            for cy in (-1, 0, 1):
                index = number(cx, cy, t % 3 - 1)
                value = fringe[index]
                for up in (0, 1):
                    value = from_side(y_in.at[up], 0, t, cy, up, 0, (1, 2), value)
                    if cx:
                        near = d_in.at[up, 0 if cx > 0 else 1]
                        first, there = (3, 0) if cx > 0 else (0, 3)
                        value = from_side(near, first, t, cy, up, -16 * cx, (there,), value)
                fringe[index] = value
        value = own_part(MASK, 0)
        for up in (0, 1):
            value = from_side(y_in.at[up], 0, NINE, 0, up, 0, (1, 2), value)
        fringe_mask[...] = value

    def lay_out(s):
        block = lane // 32
        for cz in (-1, 0, 1):
            by_cx = []
            for cx in (-1, 0, 1):
                value = fringe[number(cx, 1, cz)]
                value = jnp.where(column < 2, turn(fringe[number(cx, -1, cz)], -4), value)
                if s == STEPS - 1:
                    rest = fringe[number(cx, 0, cz)]
                    value = jnp.where(column == 4, turn(rest, -1), value)
                    value = jnp.where(column == 5, turn(rest, 3), value)
                by_cx.append(value)
            for j in range(tiles):
                parts = [turn(by_cx[b], 32 * (b - j)) for b in range(3)]
                rows = jnp.where(block == 0, parts[0], jnp.where(block == 1, parts[1], parts[2]))
                halo[cz + 1, PAD + 8 * j : PAD + 8 * j + 8, :] = rows
                if j == 0:
                    halo[cz + 1, PAD + depth : PAD + depth + 8, :] = rows
                if j == tiles - 1:
                    halo[cz + 1, 0:8, :] = rows

    def step_fringe():
        pops = []
        for index in range(27):
            cx, cz = index // 9 - 1, index % 3 - 1
            value = turn(fringe[index], 8 * cx)
            if cz:
                value = pltpu.roll(value, cz % 8, axis=0)
                value = jnp.where(line == (0 if cz > 0 else 7), turn(value, 32 * cz), value)
            pops.append(value)
        after = collide(pops)
        fluid = fringe_mask[...] == 1.0
        for index in range(27):
            value = jnp.where(fluid, after[index], pops[26 - index])
            fringe[index] = turn(value, index // 3 % 3 - 1)

    def with_ends(s, row, p, cx, cz, pops):
        if s == 0:
            return
        rows = halo[cz + 1, pl.ds(PAD + row + shift_of(s) + s - cz, 8), :]
        place = 32 * (cx + 1) + 8 * (p + 1 - cx)
        both = pltpu.roll(rows, (-place - 2) % 128, axis=1)
        low, high = number(cx, -1, cz), number(cx, 1, cz)
        pops[high] = jnp.where(lane < 2, both, pops[high])
        pops[low] = jnp.where(lane >= 126, both, pops[low])
        if s == STEPS - 1:
            both = pltpu.roll(rows, (-place - 5) % 128, axis=1)
            rest = number(cx, 0, cz)
            pops[rest] = jnp.where((lane == 0) | (lane == 127), both, pops[rest])

    def place_own(s, to):
        def body(j, carry):
            row = pl.multiple_of(8 * j, 8)
            for p in (0, 1):
                for cx in (0, 2 * p - 1):
                    for cy in (-1, 0, 1):
                        for cz in (-1, 0, 1):
                            index = number(cx, cy, cz)
                            start = PAD + row + shift_of(s) - cz
                            value = post[s, index, p + 1 - cx, pl.ds(start, 8), :]
                            if cy:
                                value = pltpu.roll(value, cy % 128, axis=1)
                            to[index, p, pl.ds(row, 8), :] = value
            return carry

        lax.fori_loop(0, tiles, body, 0)

    def place_ends(s, to):
        def body(j, carry):
            row = pl.multiple_of(8 * j, 8)
            for p in (0, 1):
                for cx in (0, 2 * p - 1):
                    for cz in (-1, 0, 1):
                        names = [number(cx, cy, cz) for cy in ((-1, 0, 1) if s == STEPS - 1 else (-1, 1))]
                        pops = {index: to[index, p, pl.ds(row, 8), :] for index in names}
                        with_ends(s, row, p, cx, cz, pops)
                        for index in names:
                            to[index, p, pl.ds(row, 8), :] = pops[index]
            return carry

        lax.fori_loop(0, tiles, body, 0)

    def place_faces(s, to):
        for up in (0, 1):
            x_copy(s, up, 0).wait_recv()
        for j in range(1, tiles + 1):
            if j < tiles:
                for up in (0, 1):
                    x_copy(s, up, j).wait_recv()
            else:
                wrap_faces(s, depth, 0)
            row = 8 * (j % tiles)
            for p in (0, 1):
                for index, value in streamed(s, p, 1 - 2 * p, row).items():
                    to[index, p, row : row + 8, :] = value

    for copy in loads:
        copy.wait()
    mask[:, depth : depth + 8, :] = mask[:, 0:8, :]
    relax(0)
    make_rim()
    make_messages()
    for index in range(27):
        fringe[index] = own_part(index, index // 3 % 3 - 1)
    pl.semaphore_wait(barrier, len(NEIGHBOURS))
    for up in (0, 1):
        for dx in (0, -1, 1):
            y_copy(up, dx).start()
    send_fringe(0)
    for j in range(tiles):
        for up in (0, 1):
            x_copy(0, up, j).start()
    place_own(0, f)
    relax(1)
    place_own(1, f)
    receive_fringe(0)
    receive_sides()
    step_fringe()
    send_fringe(1)
    receive_fringe(1)
    lay_out(1)
    step_fringe()
    send_fringe(2)
    place_ends(1, f)
    relax(2)
    place_own(2, out)
    receive_fringe(2)
    lay_out(2)
    place_ends(2, out)
    place_faces(2, out)
    for up in (0, 1):
        for dx in (-1, 0, 1):
            y_copy(up, dx).wait_send()
        for s in range(STEPS):
            e_copy(s, up).wait_send()
            for j in range(tiles):
                x_copy(s, up, j).wait_send()


def solution(mesh):
    count_x, count_y = mesh.shape["gx"], mesh.shape["gy"]

    def on_device(populations, fluid_mask):
        width_x, depth, width_y = fluid_mask.shape
        tall = depth + 2 * PAD

        def body(*refs):
            kernel(count_x, count_y, *refs)

        return pl.pallas_call(
            body,
            out_shape=pltpu.VMEM(populations.shape, jnp.float32),
            in_specs=[pl.BlockSpec(memory_space=pltpu.HBM)] * 2,
            out_specs=pl.BlockSpec(memory_space=pltpu.VMEM),
            scratch_shapes=[
                pltpu.VMEM(populations.shape, jnp.float32),
                pltpu.VMEM((width_x, depth + 8, width_y), jnp.int32),
                pltpu.VMEM((STEPS, 27, width_x + 2, tall, width_y), jnp.float32),
                pltpu.VMEM((MASK + 1, 8, 128), jnp.float32),
                pltpu.VMEM((27, 8, 128), jnp.float32),
                pltpu.VMEM((8, 128), jnp.float32),
                pltpu.VMEM((3, tall, 128), jnp.float32),
                pltpu.VMEM((2, 5, 8, 128), jnp.float32),
                pltpu.VMEM((2, 5, 8, 128), jnp.float32),
                pltpu.VMEM((2, 2, 2, 8, 128), jnp.float32),
                pltpu.VMEM((STEPS, 2, 3, 8, 128), jnp.float32),
                pltpu.VMEM((STEPS, 2, 3, 8, 128), jnp.float32),
                pltpu.SemaphoreType.DMA((2,)),
                pltpu.SemaphoreType.DMA((STEPS, 2, depth // 8)),
                pltpu.SemaphoreType.DMA((STEPS, 2, depth // 8)),
                pltpu.SemaphoreType.DMA((STEPS, 2)),
                pltpu.SemaphoreType.DMA((STEPS, 2)),
                pltpu.SemaphoreType.DMA((2, 3)),
                pltpu.SemaphoreType.DMA((2, 3)),
            ],
            compiler_params=pltpu.CompilerParams(
                collective_id=0, has_side_effects=True, vmem_limit_bytes=60 * 2**20
            ),
            cost_estimate=pl.CostEstimate(
                flops=500 * STEPS * fluid_mask.size,
                bytes_accessed=8 * populations.size,
                transcendentals=0,
            ),
            name="lattice_steps",
        )(populations, fluid_mask)

    in_specs = (P(None, "gx", None, "gy"), P("gx", None, "gy"))
    out_specs = P(None, "gx", None, "gy")
    return jax.shard_map(
        on_device, mesh=mesh, in_specs=in_specs, out_specs=out_specs, check_vma=False
    )
```

```python
import jax
import jax.numpy as jnp
from jax import lax
from jax.experimental import pallas as pl
from jax.experimental.pallas import tpu as pltpu
from jax.sharding import PartitionSpec as P

STEPS = 3
MESH = pl.DeviceIdType.MESH

shear_rate = 1.6
body_force = 0.002
keep = 1.0 - shear_rate
third = 1.0 / 3.0

PAD = 8
NINE = 9
ALONG_X = [(-1, 0), (1, 0)]
ACROSS = [(dx, dy) for dx in (-1, 0, 1) for dy in (-1, 1)]

OWN = {cy: [(cy - 4, (2 + cy, 6)), (7 + cy, (8, 12 + cy))] for cy in (-1, 0, 1)}
SENT = {
    1: {1: (-3, (0, 2), 0, (0, 2)), 0: (-1, (3, 4), -3, (0, 1)), -1: (0, (5, 5), -5, (0, 0))},
    0: {-1: (-6, (0, 2), 12, (12, 14)), 0: (-3, (3, 4), 10, (13, 14)), 1: (-1, (5, 5), 9, (14, 14))},
}
SLOTS = {(-1, -1): (0, 0), (-1, 0): (0, 1), (-1, 1): (0, 2), (0, -1): (0, 3),
         (1, -1): (1, 0), (1, 0): (1, 1), (1, 1): (1, 2), (0, 0): (1, 3),
         (0, 1): (2, 0), None: (2, 1)}
MASK = 27


def inverse_triple(zeroth, first, second, speed):
    if zeroth is None:
        raw_one = first
        raw_two = 2.0 * speed * first
        rest = -raw_two
    else:
        if first is None:
            raw_one = speed * zeroth
            raw_two = second + speed * raw_one
        else:
            raw_one = first + speed * zeroth
            raw_two = speed * (first + raw_one)
            if second is not None:
                raw_two = second + raw_two
        rest = zeroth - raw_two
    plus = 0.5 * (raw_two + raw_one)
    return plus - raw_one, rest, plus


def collide(f):
    g = [[[f[9 * a + 3 * b + c] for c in range(3)] for b in range(3)] for a in range(3)]
    even = [[g[2][b][c] + g[0][b][c] for c in range(3)] for b in range(3)]
    diff = [[g[2][b][c] - g[0][b][c] for c in range(3)] for b in range(3)]
    total = [[even[b][c] + g[1][b][c] for c in range(3)] for b in range(3)]
    t_even = [total[2][c] + total[0][c] for c in range(3)]
    t_diff = [total[2][c] - total[0][c] for c in range(3)]
    t_total = [t_even[c] + total[1][c] for c in range(3)]
    d_total = [diff[2][c] + diff[0][c] + diff[1][c] for c in range(3)]
    d_diff = [diff[2][c] - diff[0][c] for c in range(3)]
    e_total = [even[2][c] + even[0][c] + even[1][c] for c in range(3)]
    m002 = t_total[2] + t_total[0]
    jz = t_total[2] - t_total[0]
    rho = m002 + t_total[1]
    jy = t_diff[0] + t_diff[1] + t_diff[2]
    m011 = t_diff[2] - t_diff[0]
    m020 = t_even[0] + t_even[1] + t_even[2]
    jx = d_total[0] + d_total[1] + d_total[2]
    m101 = d_total[2] - d_total[0]
    m110 = d_diff[0] + d_diff[1] + d_diff[2]
    m200 = e_total[0] + e_total[1] + e_total[2]
    r = 1.0 / rho
    ux = (jx + 0.5 * body_force) * r
    uy = jy * r
    uz = jz * r
    s100 = ux * rho - jx
    s010 = uy * rho - jy
    s001 = uz * rho - jz
    k200 = m200 - ux * (jx - s100)
    k020 = m020 - uy * (jy - s010)
    k002 = m002 - uz * (jz - s001)
    k110 = m110 - ux * jy + uy * s100
    k101 = m101 - ux * jz + uz * s100
    k011 = m011 - uy * jz + uz * s010
    base = third * rho - (keep * third) * (k200 + k020 + k002)
    s200 = keep * k200 + base
    s020 = keep * k020 + base
    s002 = keep * k002 + base
    s110 = keep * k110
    s101 = keep * k101
    s011 = keep * k011
    d110 = 2.0 * s110
    d101 = 2.0 * s101
    d011 = 2.0 * s011
    q110 = d110 * s110
    q101 = d101 * s101
    q011 = d011 * s011
    p220 = s200 * s020 + q110
    s220 = p220 * r
    s202 = (s200 * s002 + q101) * r
    s022 = (s020 * s002 + q011) * r
    s211 = (s200 * s011 + d110 * s101) * r
    s121 = (s020 * s101 + d110 * s011) * r
    s112 = (s002 * s110 + d101 * s011) * r
    s222 = (p220 * s002 + q101 * s020 + q011 * s200 + 2.0 * d110 * s101 * d011) * (r * r)
    along_z = [[None] * 3 for _ in range(3)]
    along_z[0][0] = inverse_triple(rho, s001, s002, uz)
    along_z[1][0] = inverse_triple(s100, s101, None, uz)
    along_z[0][1] = inverse_triple(s010, s011, None, uz)
    along_z[2][0] = inverse_triple(s200, None, s202, uz)
    along_z[0][2] = inverse_triple(s020, None, s022, uz)
    along_z[1][1] = inverse_triple(s110, None, s112, uz)
    along_z[2][1] = inverse_triple(None, s211, None, uz)
    along_z[1][2] = inverse_triple(None, s121, None, uz)
    along_z[2][2] = inverse_triple(s220, None, s222, uz)
    out = [None] * 27
    for c in range(3):
        along_y = [
            inverse_triple(along_z[a][0][c], along_z[a][1][c], along_z[a][2][c], uy)
            for a in range(3)
        ]
        for b in range(3):
            triple = inverse_triple(along_y[0][b], along_y[1][b], along_y[2][b], ux)
            for a in range(3):
                out[9 * a + 3 * b + c] = triple[a]
    return out


def turn(value, shift):
    return pltpu.roll(value, shift % 128, axis=1) if shift % 128 else value


def number(cx, cy, cz):
    return 9 * (cx + 1) + 3 * (cy + 1) + cz + 1


def kernel(count_x, count_y, f_hbm, m_hbm, out, f, mask, post, rim, fringe, fringe_mask,
           y_out, y_in, d_in, e_out, e_in,
           ready, in_sem, x_send, x_recv, e_send, e_recv, y_send, y_recv):
    gx, gy = lax.axis_index("gx"), lax.axis_index("gy")
    depth = post.shape[3] - 2 * PAD
    tiles = depth // 8
    half = depth // 2

    def device(dx, dy):
        return (lax.rem(gx + dx + count_x, count_x), lax.rem(gy + dy + count_y, count_y))

    barrier = pltpu.get_barrier_semaphore()
    odd = lax.rem(gy, 2)

    def tell(semaphore, places):
        for dx, dy in places:
            pl.semaphore_signal(semaphore, inc=1, device_id=device(dx, dy), device_id_type=MESH)

    tell(barrier, ALONG_X)

    @pl.when(odd == 0)
    def _():
        tell(barrier, ACROSS)

    def load(j):
        rows = pl.ds(pl.multiple_of(8 * j, 8), 8)
        return pltpu.make_async_copy(f_hbm.at[:, :, rows], f.at[:, :, rows], in_sem.at[j])

    load_mask = pltpu.make_async_copy(m_hbm, mask.at[:, pl.ds(0, depth)], in_sem.at[tiles])
    load_mask.start()
    for j in range(tiles):
        load(j).start()

    lane = lax.broadcasted_iota(jnp.int32, (8, 128), 1)
    line = lax.broadcasted_iota(jnp.int32, (8, 128), 0)
    column = lane % 16
    plane = (lane // 16) % 4

    def among(lanes, planes):
        low, high = lanes
        here = (column >= low) & (column <= high) if low < high else column == low
        one = plane == planes[0]
        for other in planes[1:]:
            one = one | (plane == other)
        return here & one

    def x_copy(s, up, j):
        rows = pl.ds(PAD + half * j, half)
        lo = 18 if up else 0
        here, there = (2, 0) if up else (1, 3)
        return pltpu.make_async_remote_copy(
            src_ref=post.at[s, pl.ds(lo, NINE), here, rows],
            dst_ref=post.at[s, pl.ds(lo, NINE), there, rows],
            send_sem=x_send.at[s, up, j],
            recv_sem=x_recv.at[s, up, j],
            device_id=device(1 if up else -1, 0),
            device_id_type=MESH,
        )

    def e_copy(s, up):
        return pltpu.make_async_remote_copy(
            src_ref=e_out.at[s, up],
            dst_ref=e_in.at[s, up],
            send_sem=e_send.at[s, up],
            recv_sem=e_recv.at[s, up],
            device_id=device(1 if up else -1, 0),
            device_id_type=MESH,
        )

    def y_copy(up, dx):
        if dx:
            src, dst = y_out.at[up, (1 + dx) // 2], d_in.at[up, (1 - dx) // 2]
        else:
            src, dst = y_out.at[up], y_in.at[up]
        return pltpu.make_async_remote_copy(
            src_ref=src,
            dst_ref=dst,
            send_sem=y_send.at[up, dx + 1],
            recv_sem=y_recv.at[up, 1 - dx],
            device_id=device(dx, 1 if up else -1),
            device_id_type=MESH,
        )

    def shift_of(s):
        return 1 if s < STEPS - 1 else 1 - STEPS

    def streamed(s, p, cx, row):
        pops = {}
        for cz in (-1, 0, 1):
            for cy in (-1, 0, 1):
                value = post[s, number(cx, cy, cz), p + 1 - cx, pl.ds(PAD + row + shift_of(s) - cz, 8), :]
                if cy:
                    value = pltpu.roll(value, cy % 128, axis=1)
                pops[number(cx, cy, cz)] = value
        return pops

    def place_far(s, j):
        row = pl.multiple_of(8 * j, 8)
        for p in (0, 1):
            for index, value in streamed(s, p, 1 - 2 * p, row).items():
                f[index, p, pl.ds(row, 8), :] = value

    def relax(s, to):
        ahead = 0 if s else 0
        behind = 1 if s == STEPS - 1 else 2

        def body(j, carry):
            row = pl.multiple_of(8 * j, 8)
            again = jnp.where(j == 0, PAD + depth, jnp.where(j == tiles - 1, 0, PAD + row))
            again = pl.multiple_of(again, 8)
            if s:

                @pl.when(j == tiles // 2 - 1)
                def _():
                    for up in (0, 1):
                        x_copy(s - 1, up, 1).wait_recv()

            far = [streamed(s - 1, p, 1 - 2 * p, row) if s and not ahead else {} for p in (0, 1)]
            before = [
                [far[p][i] if i in far[p] else f[i, p, pl.ds(row, 8), :] for i in range(27)]
                for p in (0, 1)
            ]
            if ahead:
                place_far(s - 1, jnp.minimum(j + 1, tiles - 1))
            place_own(s, to, jnp.maximum(j - behind, 2 - behind))
            for p in (0, 1):
                pops = before[p]
                fluid = mask[p, pl.ds(row + s, 8), :] == 1
                after = collide(pops)
                for index in range(27):
                    value = jnp.where(fluid, after[index], pops[26 - index])
                    post[s, index, p + 1, pl.ds(PAD + row, 8), :] = value
                    post[s, index, p + 1, pl.ds(again, 8), :] = value
            if s:

                @pl.when(j % (tiles // 2) == tiles // 2 - 1)
                def _():
                    for up in (0, 1):
                        x_copy(s, up, j // (tiles // 2)).start()

            return carry

        if s:
            for up in (0, 1):
                x_copy(s - 1, up, 0).wait_recv()
            wrap_faces(s - 1, PAD, PAD + depth)
            if ahead:
                place_far(s - 1, 0)
        lax.fori_loop(0, tiles, body, 0)

    def finish_own(s, to):
        def body(k, carry):
            j = lax.rem(tiles - 1 + k, tiles) if s == STEPS - 1 else tiles - 2 + k
            place_own(s, to, j)
            return carry

        lax.fori_loop(0, 2, body, 0)

    def wrap_faces(s, start, end):
        for there, lo in ((0, 18), (3, 0)):
            for index in range(lo, lo + NINE):
                post[s, index, there, end : end + 8, :] = post[s, index, there, start : start + 8, :]

    def make_rim():
        def gather(index, tile):
            for v in (0, 1):
                packed = None
                for low in (0, 1):
                    for p in (0, 1):
                        start = 64 * low + 16 * (p + 1)
                        value = turn(tile(2 * v + low, p), start - 122)
                        here = (lane >= start) & (lane < start + 16)
                        packed = value if packed is None else jnp.where(here, value, packed)
                rim[index, v] = packed

        def body(third, carry):
            for k in range(3):
                index = 3 * third + k
                gather(index, lambda j, p: f[index, p, 8 * j : 8 * j + 8, :])
            return carry

        lax.fori_loop(0, NINE, body, 0)
        gather(MASK, lambda j, p: mask[p, 8 * j : 8 * j + 8, :].astype(jnp.float32))
        for v in (0, 1):
            pops = [rim[index, v] for index in range(27)]
            after = collide(pops)
            fluid = rim[MASK, v] == 1.0
            for index in range(27):
                rim[index, v] = jnp.where(fluid, after[index], pops[26 - index])

    def own_part(index, cy, v):
        value = None
        for shift, lanes in OWN[cy]:
            moved = turn(rim[index, v], shift)
            value = moved if value is None else jnp.where(among(lanes, (1, 2)), moved, value)
        return value

    def make_messages():
        for up in (0, 1):
            packed = [[jnp.zeros((8, 128), jnp.float32)] * 2 for _ in range(3)]
            for what, (pair, quarter) in SLOTS.items():
                right, around = quarter % 2, quarter // 2
                for cy in (-1, 0, 1):
                    if what is None and cy:
                        continue
                    index = number(what[0], cy, what[1]) if what else MASK
                    shift, (low, high), _, _ = SENT[up][cy]
                    here = among((low + 8 * right, high + 8 * right), (3, 0) if around else (1, 2))
                    for v in (0, 1):
                        value = turn(rim[index, v], shift + 8 * right + 32 * around)
                        packed[pair][v] = jnp.where(here, value, packed[pair][v])
            for pair in range(3):
                for v in (0, 1):
                    y_out[up, pair, v] = packed[pair][v]

    def from_side(tile, what, cy, up, across, planes, value):
        quarter = SLOTS[what][1]
        _, _, shift, lanes = SENT[up][cy]
        moved = turn(tile, shift - 8 * (quarter % 2) - 32 * (quarter // 2) + across)
        return jnp.where(among(lanes, planes), moved, value)

    def send_fringe(s):
        for up in (0, 1):
            for pair in range(3):
                for v in (0, 1):
                    packed = None
                    for q in range(4 * pair, min(4 * pair + 4, NINE)):
                        value = turn(fringe[18 * up + q, v], 16 * (q % 4 - 1 - up))
                        packed = value if packed is None else jnp.where(plane == q % 4, value, packed)
                    e_out[s, up, pair, v] = packed
            e_copy(s, up).start()

    def receive_fringe(s):
        for up in (0, 1):
            e_copy(s, up).wait_recv()
            there = 0 if up else 3
            for q in range(NINE):
                index = 18 * up + q
                for v in (0, 1):
                    moved = turn(e_in[s, up, q // 4, v], 16 * (there - q % 4))
                    fringe[index, v] = jnp.where(plane == there, moved, fringe[index, v])

    def receive_sides():
        for up in (0, 1):
            for dx in (-1, 0, 1):
                y_copy(up, dx).wait_recv()
        for v in (0, 1):
            for what, (pair, _) in SLOTS.items():
                if what is None:
                    value = own_part(MASK, 0, v)
                    for up in (0, 1):
                        value = from_side(y_in[up, pair, v], what, 0, up, 0, (1, 2), value)
                    fringe_mask[v] = value
                    continue
                cx, cz = what
                for cy in (-1, 0, 1):
                    value = fringe[number(cx, cy, cz), v]
                    for up in (0, 1):
                        value = from_side(y_in[up, pair, v], what, cy, up, 0, (1, 2), value)
                        if cx:
                            near, there = (0, 0) if cx > 0 else (1, 3)
                            value = from_side(d_in[up, near, v], what, cy, up, -32 * cx, (there,), value)
                    fringe[number(cx, cy, cz), v] = value

    def moved_fringe(index):
        cx, cz = index // 9 - 1, index % 3 - 1
        pair = [turn(fringe[index, v], 16 * cx) for v in (0, 1)]
        if cz == 0:
            return pair
        pair = [pltpu.roll(value, cz % 8, axis=0) for value in pair]
        other = [turn(value, 64) for value in pair]
        first, second = (other[::-1], other) if cz > 0 else (other, other[::-1])
        edge = line == (0 if cz > 0 else 7)
        return [
            jnp.where(edge, jnp.where(lane < 64, first[v], second[v]), pair[v]) for v in (0, 1)
        ]

    def step_fringe():
        pops = [moved_fringe(index) for index in range(27)]
        for v in (0, 1):
            before = [pair[v] for pair in pops]
            after = collide(before)
            fluid = fringe_mask[v] == 1.0
            for index in range(27):
                value = jnp.where(fluid, after[index], before[26 - index])
                fringe[index, v] = turn(value, index // 3 % 3 - 1)

    def place_fringe(far):
        for index in range(27):
            cx = index // 9 - 1
            planes = [p for p in (0, 1) if (cx == 1 - 2 * p) == far]
            if not planes:
                continue
            pair = moved_fringe(index)
            for j in range(tiles):
                for p in planes:
                    start = 64 * (j % 2) + 16 * (p + 1)
                    left = turn(pair[j // 2], -start - 2)
                    right = turn(pair[j // 2], 125 - start - 10)
                    value = out[index, p, 8 * j : 8 * j + 8, :]
                    value = jnp.where(lane < 3, left, jnp.where(lane >= 125, right, value))
                    out[index, p, 8 * j : 8 * j + 8, :] = value

    def place_own(s, to, j):
        row = pl.multiple_of(8 * j, 8)
        for p in (0, 1):
            for cx in (0, 2 * p - 1):
                for cy in (-1, 0, 1):
                    for cz in (-1, 0, 1):
                        index = number(cx, cy, cz)
                        start = PAD + row + shift_of(s) - cz
                        value = post[s, index, p + 1 - cx, pl.ds(start, 8), :]
                        if cy:
                            value = pltpu.roll(value, cy % 128, axis=1)
                        to[index, p, pl.ds(row, 8), :] = value

    def place_faces(s, to):
        for up in (0, 1):
            x_copy(s, up, 0).wait_recv()
        for j in range(1, tiles + 1):
            if j == tiles // 2:
                for up in (0, 1):
                    x_copy(s, up, 1).wait_recv()
            if j == tiles:
                wrap_faces(s, depth, 0)
            row = 8 * (j % tiles)
            for p in (0, 1):
                for index, value in streamed(s, p, 1 - 2 * p, row).items():
                    to[index, p, row : row + 8, :] = value

    load_mask.wait()
    mask[:, depth : depth + 8, :] = mask[:, 0:8, :]
    for j in range(tiles):
        load(j).wait()
    make_rim()
    make_messages()

    def send_sides():
        for up in (0, 1):
            for dx in (0, -1, 1):
                y_copy(up, dx).start()

    @pl.when(odd == 1)
    def _():
        pl.semaphore_wait(barrier, len(ALONG_X) + len(ACROSS))
        tell(ready, ACROSS)
        send_sides()

    relax(0, f)

    @pl.when(odd == 0)
    def _():
        pl.semaphore_wait(barrier, len(ALONG_X))

    for index in range(27):
        for v in (0, 1):
            fringe[index, v] = own_part(index, index // 3 % 3 - 1, v)
    for j in (0, 1):
        for up in (0, 1):
            x_copy(0, up, j).start()
    send_fringe(0)
    finish_own(0, f)
    relax(1, f)
    finish_own(1, f)

    @pl.when(odd == 0)
    def _():
        pl.semaphore_wait(ready, len(ACROSS))
        send_sides()

    receive_fringe(0)
    receive_sides()
    step_fringe()
    send_fringe(1)
    relax(2, out)
    receive_fringe(1)
    step_fringe()
    send_fringe(2)
    finish_own(2, out)
    place_fringe(False)
    for up in (0, 1):
        for dx in (-1, 0, 1):
            y_copy(up, dx).wait_send()
        for s in range(STEPS):
            e_copy(s, up).wait_send()
            for j in (0, 1):
                x_copy(s, up, j).wait_send()
    place_faces(2, out)
    receive_fringe(2)
    place_fringe(True)


def solution(mesh):
    count_x, count_y = mesh.shape["gx"], mesh.shape["gy"]

    def on_device(populations, fluid_mask):
        width_x, depth, width_y = fluid_mask.shape
        tall = depth + 2 * PAD

        def body(*refs):
            kernel(count_x, count_y, *refs)

        return pl.pallas_call(
            body,
            out_shape=pltpu.VMEM(populations.shape, jnp.float32),
            in_specs=[pl.BlockSpec(memory_space=pltpu.HBM)] * 2,
            out_specs=pl.BlockSpec(memory_space=pltpu.VMEM),
            scratch_shapes=[
                pltpu.VMEM(populations.shape, jnp.float32),
                pltpu.VMEM((width_x, depth + 8, width_y), jnp.int32),
                pltpu.VMEM((STEPS, 27, width_x + 2, tall, width_y), jnp.float32),
                pltpu.VMEM((MASK + 1, 2, 8, 128), jnp.float32),
                pltpu.VMEM((27, 2, 8, 128), jnp.float32),
                pltpu.VMEM((2, 8, 128), jnp.float32),
                pltpu.VMEM((2, 3, 2, 8, 128), jnp.float32),
                pltpu.VMEM((2, 3, 2, 8, 128), jnp.float32),
                pltpu.VMEM((2, 2, 2, 8, 128), jnp.float32),
                pltpu.VMEM((STEPS, 2, 3, 2, 8, 128), jnp.float32),
                pltpu.VMEM((STEPS, 2, 3, 2, 8, 128), jnp.float32),
                pltpu.SemaphoreType.REGULAR,
                pltpu.SemaphoreType.DMA((depth // 8 + 1,)),
                pltpu.SemaphoreType.DMA((STEPS, 2, 2)),
                pltpu.SemaphoreType.DMA((STEPS, 2, 2)),
                pltpu.SemaphoreType.DMA((STEPS, 2)),
                pltpu.SemaphoreType.DMA((STEPS, 2)),
                pltpu.SemaphoreType.DMA((2, 3)),
                pltpu.SemaphoreType.DMA((2, 3)),
            ],
            compiler_params=pltpu.CompilerParams(
                collective_id=0, has_side_effects=True, vmem_limit_bytes=60 * 2**20
            ),
            cost_estimate=pl.CostEstimate(
                flops=500 * STEPS * fluid_mask.size,
                bytes_accessed=8 * populations.size,
                transcendentals=0,
            ),
            name="lattice_steps",
        )(populations, fluid_mask)

    in_specs = (P(None, "gx", None, "gy"), P("gx", None, "gy"))
    out_specs = P(None, "gx", None, "gy")
    return jax.shard_map(
        on_device, mesh=mesh, in_specs=in_specs, out_specs=out_specs, check_vma=False
    )
```

```python
import jax
import jax.numpy as jnp
from jax import lax
from jax.experimental import pallas as pl
from jax.experimental.pallas import tpu as pltpu
from jax.sharding import PartitionSpec as P

STEPS = 3
MESH = pl.DeviceIdType.MESH

shear_rate = 1.6
body_force = 0.002
keep = 1.0 - shear_rate
third = 1.0 / 3.0

PAD = 8
NINE = 9
ALONG_X = [(-1, 0), (1, 0)]
ACROSS = [(dx, dy) for dx in (-1, 0, 1) for dy in (-1, 1)]

OWN = {cy: [(cy - 4, (2 + cy, 6)), (7 + cy, (8, 12 + cy))] for cy in (-1, 0, 1)}
SENT = {
    1: {1: (-3, (0, 2), 0, (0, 2)), 0: (-1, (3, 4), -3, (0, 1)), -1: (0, (5, 5), -5, (0, 0))},
    0: {-1: (-6, (0, 2), 12, (12, 14)), 0: (-3, (3, 4), 10, (13, 14)), 1: (-1, (5, 5), 9, (14, 14))},
}
SLOTS = {(-1, -1): (0, 0), (-1, 0): (0, 1), (-1, 1): (0, 2), (0, -1): (0, 3),
         (1, -1): (1, 0), (1, 0): (1, 1), (1, 1): (1, 2), (0, 0): (1, 3),
         (0, 1): (2, 0), None: (2, 1)}
MASK = 27


def inverse_triple(zeroth, first, second, speed):
    if zeroth is None:
        raw_one = first
        raw_two = 2.0 * speed * first
        rest = -raw_two
    else:
        if first is None:
            raw_one = speed * zeroth
            raw_two = second + speed * raw_one
        else:
            raw_one = first + speed * zeroth
            raw_two = speed * (first + raw_one)
            if second is not None:
                raw_two = second + raw_two
        rest = zeroth - raw_two
    plus = 0.5 * (raw_two + raw_one)
    return plus - raw_one, rest, plus


def collide(f):
    g = [[[f[9 * a + 3 * b + c] for c in range(3)] for b in range(3)] for a in range(3)]
    even = [[g[2][b][c] + g[0][b][c] for c in range(3)] for b in range(3)]
    diff = [[g[2][b][c] - g[0][b][c] for c in range(3)] for b in range(3)]
    total = [[even[b][c] + g[1][b][c] for c in range(3)] for b in range(3)]
    t_even = [total[2][c] + total[0][c] for c in range(3)]
    t_diff = [total[2][c] - total[0][c] for c in range(3)]
    t_total = [t_even[c] + total[1][c] for c in range(3)]
    d_total = [diff[2][c] + diff[0][c] + diff[1][c] for c in range(3)]
    d_diff = [diff[2][c] - diff[0][c] for c in range(3)]
    e_total = [even[2][c] + even[0][c] + even[1][c] for c in range(3)]
    m002 = t_total[2] + t_total[0]
    jz = t_total[2] - t_total[0]
    rho = m002 + t_total[1]
    jy = t_diff[0] + t_diff[1] + t_diff[2]
    m011 = t_diff[2] - t_diff[0]
    m020 = t_even[0] + t_even[1] + t_even[2]
    jx = d_total[0] + d_total[1] + d_total[2]
    m101 = d_total[2] - d_total[0]
    m110 = d_diff[0] + d_diff[1] + d_diff[2]
    m200 = e_total[0] + e_total[1] + e_total[2]
    r = 1.0 / rho
    ux = (jx + 0.5 * body_force) * r
    uy = jy * r
    uz = jz * r
    s100 = ux * rho - jx
    s010 = uy * rho - jy
    s001 = uz * rho - jz
    k200 = m200 - ux * (jx - s100)
    k020 = m020 - uy * (jy - s010)
    k002 = m002 - uz * (jz - s001)
    k110 = m110 - ux * jy + uy * s100
    k101 = m101 - ux * jz + uz * s100
    k011 = m011 - uy * jz + uz * s010
    base = third * rho - (keep * third) * (k200 + k020 + k002)
    s200 = keep * k200 + base
    s020 = keep * k020 + base
    s002 = keep * k002 + base
    s110 = keep * k110
    s101 = keep * k101
    s011 = keep * k011
    d110 = 2.0 * s110
    d101 = 2.0 * s101
    d011 = 2.0 * s011
    q110 = d110 * s110
    q101 = d101 * s101
    q011 = d011 * s011
    p220 = s200 * s020 + q110
    s220 = p220 * r
    s202 = (s200 * s002 + q101) * r
    s022 = (s020 * s002 + q011) * r
    s211 = (s200 * s011 + d110 * s101) * r
    s121 = (s020 * s101 + d110 * s011) * r
    s112 = (s002 * s110 + d101 * s011) * r
    s222 = (p220 * s002 + q101 * s020 + q011 * s200 + 2.0 * d110 * s101 * d011) * (r * r)
    along_z = [[None] * 3 for _ in range(3)]
    along_z[0][0] = inverse_triple(rho, s001, s002, uz)
    along_z[1][0] = inverse_triple(s100, s101, None, uz)
    along_z[0][1] = inverse_triple(s010, s011, None, uz)
    along_z[2][0] = inverse_triple(s200, None, s202, uz)
    along_z[0][2] = inverse_triple(s020, None, s022, uz)
    along_z[1][1] = inverse_triple(s110, None, s112, uz)
    along_z[2][1] = inverse_triple(None, s211, None, uz)
    along_z[1][2] = inverse_triple(None, s121, None, uz)
    along_z[2][2] = inverse_triple(s220, None, s222, uz)
    out = [None] * 27
    for c in range(3):
        along_y = [
            inverse_triple(along_z[a][0][c], along_z[a][1][c], along_z[a][2][c], uy)
            for a in range(3)
        ]
        for b in range(3):
            triple = inverse_triple(along_y[0][b], along_y[1][b], along_y[2][b], ux)
            for a in range(3):
                out[9 * a + 3 * b + c] = triple[a]
    return out


def turn(value, shift):
    return pltpu.roll(value, shift % 128, axis=1) if shift % 128 else value


def number(cx, cy, cz):
    return 9 * (cx + 1) + 3 * (cy + 1) + cz + 1


def kernel(count_x, count_y, f_hbm, m_hbm, out, f, mask, post, rim, fringe, fringe_mask,
           y_out, y_in, d_in, e_out, e_in,
           ready, in_sem, x_send, x_recv, e_send, e_recv, y_send, y_recv):
    gx, gy = lax.axis_index("gx"), lax.axis_index("gy")
    depth = post.shape[3] - 2 * PAD
    tiles = depth // 8
    half = depth // 2

    def device(dx, dy):
        return (lax.rem(gx + dx + count_x, count_x), lax.rem(gy + dy + count_y, count_y))

    barrier = pltpu.get_barrier_semaphore()
    odd = lax.rem(gy, 2)

    def tell(semaphore, places):
        for dx, dy in places:
            pl.semaphore_signal(semaphore, inc=1, device_id=device(dx, dy), device_id_type=MESH)

    tell(barrier, ALONG_X)

    @pl.when(odd == 0)
    def _():
        tell(barrier, ACROSS)

    def load(j):
        rows = pl.ds(pl.multiple_of(8 * j, 8), 8)
        return pltpu.make_async_copy(f_hbm.at[:, :, rows], f.at[:, :, rows], in_sem.at[j])

    load_mask = pltpu.make_async_copy(m_hbm, mask.at[:, pl.ds(0, depth)], in_sem.at[tiles])
    load_mask.start()
    for j in range(tiles):
        load(j).start()

    lane = lax.broadcasted_iota(jnp.int32, (8, 128), 1)
    line = lax.broadcasted_iota(jnp.int32, (8, 128), 0)
    column = lane % 16
    plane = (lane // 16) % 4

    def among(lanes, planes):
        low, high = lanes
        here = (column >= low) & (column <= high) if low < high else column == low
        one = plane == planes[0]
        for other in planes[1:]:
            one = one | (plane == other)
        return here & one

    def x_copy(s, up, j):
        rows = pl.ds(PAD + half * j, half)
        lo = 18 if up else 0
        here, there = (2, 0) if up else (1, 3)
        return pltpu.make_async_remote_copy(
            src_ref=post.at[s, pl.ds(lo, NINE), here, rows],
            dst_ref=post.at[s, pl.ds(lo, NINE), there, rows],
            send_sem=x_send.at[s, up, j],
            recv_sem=x_recv.at[s, up, j],
            device_id=device(1 if up else -1, 0),
            device_id_type=MESH,
        )

    def e_copy(s, up):
        return pltpu.make_async_remote_copy(
            src_ref=e_out.at[s, up],
            dst_ref=e_in.at[s, up],
            send_sem=e_send.at[s, up],
            recv_sem=e_recv.at[s, up],
            device_id=device(1 if up else -1, 0),
            device_id_type=MESH,
        )

    def y_copy(up, dx):
        if dx:
            src, dst = y_out.at[up, (1 + dx) // 2], d_in.at[up, (1 - dx) // 2]
        else:
            src, dst = y_out.at[up], y_in.at[up]
        return pltpu.make_async_remote_copy(
            src_ref=src,
            dst_ref=dst,
            send_sem=y_send.at[up, dx + 1],
            recv_sem=y_recv.at[up, 1 - dx],
            device_id=device(dx, 1 if up else -1),
            device_id_type=MESH,
        )

    def shift_of(s):
        return 1 if s < STEPS - 1 else 1 - STEPS

    def streamed(s, p, cx, row):
        pops = {}
        for cz in (-1, 0, 1):
            for cy in (-1, 0, 1):
                value = post[s, number(cx, cy, cz), p + 1 - cx, pl.ds(PAD + row + shift_of(s) - cz, 8), :]
                if cy:
                    value = pltpu.roll(value, cy % 128, axis=1)
                pops[number(cx, cy, cz)] = value
        return pops

    def place_far(s, j):
        row = pl.multiple_of(8 * j, 8)
        for p in (0, 1):
            for index, value in streamed(s, p, 1 - 2 * p, row).items():
                f[index, p, pl.ds(row, 8), :] = value

    def relax(s, to):
        ahead = 0 if s else 0
        behind = 1 if s == STEPS - 1 else 2

        def body(j, carry):
            row = pl.multiple_of(8 * j, 8)
            again = jnp.where(j == 0, PAD + depth, jnp.where(j == tiles - 1, 0, PAD + row))
            again = pl.multiple_of(again, 8)
            if s:

                @pl.when(j == tiles // 2 - 1)
                def _():
                    for up in (0, 1):
                        x_copy(s - 1, up, 1).wait_recv()

            far = [streamed(s - 1, p, 1 - 2 * p, row) if s and not ahead else {} for p in (0, 1)]
            before = [
                [far[p][i] if i in far[p] else f[i, p, pl.ds(row, 8), :] for i in range(27)]
                for p in (0, 1)
            ]
            if ahead:
                place_far(s - 1, jnp.minimum(j + 1, tiles - 1))
            place_own(s, to, jnp.maximum(j - behind, 2 - behind))
            for p in (0, 1):
                pops = before[p]
                fluid = mask[p, pl.ds(row + s, 8), :] == 1
                after = collide(pops)
                for index in range(27):
                    value = jnp.where(fluid, after[index], pops[26 - index])
                    post[s, index, p + 1, pl.ds(PAD + row, 8), :] = value
                    post[s, index, p + 1, pl.ds(again, 8), :] = value
            if s:

                @pl.when(j % (tiles // 2) == tiles // 2 - 1)
                def _():
                    for up in (0, 1):
                        x_copy(s, up, j // (tiles // 2)).start()

            return carry

        if s:
            for up in (0, 1):
                x_copy(s - 1, up, 0).wait_recv()
            wrap_faces(s - 1, PAD, PAD + depth)
            if ahead:
                place_far(s - 1, 0)
        lax.fori_loop(0, tiles, body, 0)

    def finish_own(s, to):
        def body(k, carry):
            j = lax.rem(tiles - 1 + k, tiles) if s == STEPS - 1 else tiles - 2 + k
            place_own(s, to, j)
            return carry

        lax.fori_loop(0, 2, body, 0)

    def wrap_faces(s, start, end):
        for there, lo in ((0, 18), (3, 0)):
            for index in range(lo, lo + NINE):
                post[s, index, there, end : end + 8, :] = post[s, index, there, start : start + 8, :]

    def make_rim():
        def gather(index, tile):
            for v in (0, 1):
                packed = None
                for low in (0, 1):
                    for p in (0, 1):
                        start = 64 * low + 16 * (p + 1)
                        value = turn(tile(2 * v + low, p), start - 122)
                        here = (lane >= start) & (lane < start + 16)
                        packed = value if packed is None else jnp.where(here, value, packed)
                rim[index, v] = packed

        def body(third, carry):
            for k in range(3):
                index = 3 * third + k
                gather(index, lambda j, p: f[index, p, 8 * j : 8 * j + 8, :])
            return carry

        lax.fori_loop(0, NINE, body, 0)
        gather(MASK, lambda j, p: mask[p, 8 * j : 8 * j + 8, :].astype(jnp.float32))
        for v in (0, 1):
            pops = [rim[index, v] for index in range(27)]
            after = collide(pops)
            fluid = rim[MASK, v] == 1.0
            for index in range(27):
                rim[index, v] = jnp.where(fluid, after[index], pops[26 - index])

    def own_part(index, cy, v):
        value = None
        for shift, lanes in OWN[cy]:
            moved = turn(rim[index, v], shift)
            value = moved if value is None else jnp.where(among(lanes, (1, 2)), moved, value)
        return value

    def make_messages():
        for up in (0, 1):
            packed = [[jnp.zeros((8, 128), jnp.float32)] * 2 for _ in range(3)]
            for what, (pair, quarter) in SLOTS.items():
                right, around = quarter % 2, quarter // 2
                for cy in (-1, 0, 1):
                    if what is None and cy:
                        continue
                    index = number(what[0], cy, what[1]) if what else MASK
                    shift, (low, high), _, _ = SENT[up][cy]
                    here = among((low + 8 * right, high + 8 * right), (3, 0) if around else (1, 2))
                    for v in (0, 1):
                        value = turn(rim[index, v], shift + 8 * right + 32 * around)
                        packed[pair][v] = jnp.where(here, value, packed[pair][v])
            for pair in range(3):
                for v in (0, 1):
                    y_out[up, pair, v] = packed[pair][v]

    def from_side(tile, what, cy, up, across, planes, value):
        quarter = SLOTS[what][1]
        _, _, shift, lanes = SENT[up][cy]
        moved = turn(tile, shift - 8 * (quarter % 2) - 32 * (quarter // 2) + across)
        return jnp.where(among(lanes, planes), moved, value)

    def send_fringe(s):
        for up in (0, 1):
            for pair in range(3):
                for v in (0, 1):
                    packed = None
                    for q in range(4 * pair, min(4 * pair + 4, NINE)):
                        value = turn(fringe[18 * up + q, v], 16 * (q % 4 - 1 - up))
                        packed = value if packed is None else jnp.where(plane == q % 4, value, packed)
                    e_out[s, up, pair, v] = packed
            e_copy(s, up).start()

    def receive_fringe(s):
        for up in (0, 1):
            e_copy(s, up).wait_recv()
            there = 0 if up else 3
            for q in range(NINE):
                index = 18 * up + q
                for v in (0, 1):
                    moved = turn(e_in[s, up, q // 4, v], 16 * (there - q % 4))
                    fringe[index, v] = jnp.where(plane == there, moved, fringe[index, v])

    def receive_sides():
        for up in (0, 1):
            for dx in (-1, 0, 1):
                y_copy(up, dx).wait_recv()
        for v in (0, 1):
            for what, (pair, _) in SLOTS.items():
                if what is None:
                    value = own_part(MASK, 0, v)
                    for up in (0, 1):
                        value = from_side(y_in[up, pair, v], what, 0, up, 0, (1, 2), value)
                    fringe_mask[v] = value
                    continue
                cx, cz = what
                for cy in (-1, 0, 1):
                    value = fringe[number(cx, cy, cz), v]
                    for up in (0, 1):
                        value = from_side(y_in[up, pair, v], what, cy, up, 0, (1, 2), value)
                        if cx:
                            near, there = (0, 0) if cx > 0 else (1, 3)
                            value = from_side(d_in[up, near, v], what, cy, up, -32 * cx, (there,), value)
                    fringe[number(cx, cy, cz), v] = value

    def moved_fringe(index):
        cx, cz = index // 9 - 1, index % 3 - 1
        pair = [turn(fringe[index, v], 16 * cx) for v in (0, 1)]
        if cz == 0:
            return pair
        pair = [pltpu.roll(value, cz % 8, axis=0) for value in pair]
        other = [turn(value, 64) for value in pair]
        first, second = (other[::-1], other) if cz > 0 else (other, other[::-1])
        edge = line == (0 if cz > 0 else 7)
        return [
            jnp.where(edge, jnp.where(lane < 64, first[v], second[v]), pair[v]) for v in (0, 1)
        ]

    def step_fringe():
        pops = [moved_fringe(index) for index in range(27)]
        for v in (0, 1):
            before = [pair[v] for pair in pops]
            after = collide(before)
            fluid = fringe_mask[v] == 1.0
            for index in range(27):
                value = jnp.where(fluid, after[index], before[26 - index])
                fringe[index, v] = turn(value, index // 3 % 3 - 1)

    def place_fringe(far):
        for index in range(27):
            cx = index // 9 - 1
            planes = [p for p in (0, 1) if (cx == 1 - 2 * p) == far]
            if not planes:
                continue
            pair = moved_fringe(index)
            for j in range(tiles):
                for p in planes:
                    start = 64 * (j % 2) + 16 * (p + 1)
                    left = turn(pair[j // 2], -start - 2)
                    right = turn(pair[j // 2], 125 - start - 10)
                    value = out[index, p, 8 * j : 8 * j + 8, :]
                    value = jnp.where(lane < 3, left, jnp.where(lane >= 125, right, value))
                    out[index, p, 8 * j : 8 * j + 8, :] = value

    def place_own(s, to, j):
        row = pl.multiple_of(8 * j, 8)
        for p in (0, 1):
            for cx in (0, 2 * p - 1):
                for cy in (-1, 0, 1):
                    for cz in (-1, 0, 1):
                        index = number(cx, cy, cz)
                        start = PAD + row + shift_of(s) - cz
                        value = post[s, index, p + 1 - cx, pl.ds(start, 8), :]
                        if cy:
                            value = pltpu.roll(value, cy % 128, axis=1)
                        to[index, p, pl.ds(row, 8), :] = value

    def place_faces(s, to):
        for up in (0, 1):
            x_copy(s, up, 0).wait_recv()
        for j in range(1, tiles + 1):
            if j == tiles // 2:
                for up in (0, 1):
                    x_copy(s, up, 1).wait_recv()
            if j == tiles:
                wrap_faces(s, depth, 0)
            row = 8 * (j % tiles)
            for p in (0, 1):
                for index, value in streamed(s, p, 1 - 2 * p, row).items():
                    to[index, p, row : row + 8, :] = value

    load_mask.wait()
    mask[:, depth : depth + 8, :] = mask[:, 0:8, :]
    for j in range(tiles):
        load(j).wait()
    make_rim()
    make_messages()

    def send_sides():
        for up in (0, 1):
            for dx in (0, -1, 1):
                y_copy(up, dx).start()

    @pl.when(odd == 1)
    def _():
        pl.semaphore_wait(barrier, len(ALONG_X) + len(ACROSS))
        tell(ready, ACROSS)
        send_sides()

    relax(0, f)

    @pl.when(odd == 0)
    def _():
        pl.semaphore_wait(barrier, len(ALONG_X))

    for j in (0, 1):
        for up in (0, 1):
            x_copy(0, up, j).start()
    for index in range(27):
        for v in (0, 1):
            fringe[index, v] = own_part(index, index // 3 % 3 - 1, v)
    send_fringe(0)
    finish_own(0, f)
    relax(1, f)
    finish_own(1, f)

    @pl.when(odd == 0)
    def _():
        pl.semaphore_wait(ready, len(ACROSS))
        send_sides()

    receive_fringe(0)
    receive_sides()
    step_fringe()
    send_fringe(1)
    relax(2, out)
    receive_fringe(1)
    step_fringe()
    send_fringe(2)
    finish_own(2, out)
    place_fringe(False)
    for up in (0, 1):
        for dx in (-1, 0, 1):
            y_copy(up, dx).wait_send()
        for s in range(STEPS):
            e_copy(s, up).wait_send()
            for j in (0, 1):
                x_copy(s, up, j).wait_send()
    place_faces(2, out)
    receive_fringe(2)
    place_fringe(True)


def solution(mesh):
    count_x, count_y = mesh.shape["gx"], mesh.shape["gy"]

    def on_device(populations, fluid_mask):
        width_x, depth, width_y = fluid_mask.shape
        tall = depth + 2 * PAD

        def body(*refs):
            kernel(count_x, count_y, *refs)

        return pl.pallas_call(
            body,
            out_shape=pltpu.VMEM(populations.shape, jnp.float32),
            in_specs=[pl.BlockSpec(memory_space=pltpu.HBM)] * 2,
            out_specs=pl.BlockSpec(memory_space=pltpu.VMEM),
            scratch_shapes=[
                pltpu.VMEM(populations.shape, jnp.float32),
                pltpu.VMEM((width_x, depth + 8, width_y), jnp.int32),
                pltpu.VMEM((STEPS, 27, width_x + 2, tall, width_y), jnp.float32),
                pltpu.VMEM((MASK + 1, 2, 8, 128), jnp.float32),
                pltpu.VMEM((27, 2, 8, 128), jnp.float32),
                pltpu.VMEM((2, 8, 128), jnp.float32),
                pltpu.VMEM((2, 3, 2, 8, 128), jnp.float32),
                pltpu.VMEM((2, 3, 2, 8, 128), jnp.float32),
                pltpu.VMEM((2, 2, 2, 8, 128), jnp.float32),
                pltpu.VMEM((STEPS, 2, 3, 2, 8, 128), jnp.float32),
                pltpu.VMEM((STEPS, 2, 3, 2, 8, 128), jnp.float32),
                pltpu.SemaphoreType.REGULAR,
                pltpu.SemaphoreType.DMA((depth // 8 + 1,)),
                pltpu.SemaphoreType.DMA((STEPS, 2, 2)),
                pltpu.SemaphoreType.DMA((STEPS, 2, 2)),
                pltpu.SemaphoreType.DMA((STEPS, 2)),
                pltpu.SemaphoreType.DMA((STEPS, 2)),
                pltpu.SemaphoreType.DMA((2, 3)),
                pltpu.SemaphoreType.DMA((2, 3)),
            ],
            compiler_params=pltpu.CompilerParams(
                collective_id=0, has_side_effects=True, vmem_limit_bytes=60 * 2**20
            ),
            cost_estimate=pl.CostEstimate(
                flops=500 * STEPS * fluid_mask.size,
                bytes_accessed=8 * populations.size,
                transcendentals=0,
            ),
            name="lattice_steps",
        )(populations, fluid_mask)

    in_specs = (P(None, "gx", None, "gy"), P("gx", None, "gy"))
    out_specs = P(None, "gx", None, "gy")
    return jax.shard_map(
        on_device, mesh=mesh, in_specs=in_specs, out_specs=out_specs, check_vma=False
    )
```

```python
import jax
import jax.numpy as jnp
from jax import lax
from jax.experimental import pallas as pl
from jax.experimental.pallas import tpu as pltpu
from jax.sharding import PartitionSpec as P

STEPS = 3
MESH = pl.DeviceIdType.MESH

shear_rate = 1.6
body_force = 0.002
keep = 1.0 - shear_rate
third = 1.0 / 3.0

PAD = 8
NINE = 9
ALONG_X = [(-1, 0), (1, 0)]
ACROSS = [(dx, dy) for dx in (-1, 0, 1) for dy in (-1, 1)]

OWN = {cy: [(cy - 4, (2 + cy, 6)), (7 + cy, (8, 12 + cy))] for cy in (-1, 0, 1)}
SENT = {
    1: {1: (-3, (0, 2), 0, (0, 2)), 0: (-1, (3, 4), -3, (0, 1)), -1: (0, (5, 5), -5, (0, 0))},
    0: {-1: (-6, (0, 2), 12, (12, 14)), 0: (-3, (3, 4), 10, (13, 14)), 1: (-1, (5, 5), 9, (14, 14))},
}
SLOTS = {(-1, -1): (0, 0), (-1, 0): (0, 1), (-1, 1): (0, 2), (0, -1): (0, 3),
         (1, -1): (1, 0), (1, 0): (1, 1), (1, 1): (1, 2), (0, 0): (1, 3),
         (0, 1): (2, 0), None: (2, 1)}
MASK = 27


def inverse_triple(zeroth, first, second, speed):
    if zeroth is None:
        raw_one = first
        raw_two = 2.0 * speed * first
        rest = -raw_two
    else:
        if first is None:
            raw_one = speed * zeroth
            raw_two = second + speed * raw_one
        else:
            raw_one = first + speed * zeroth
            raw_two = speed * (first + raw_one)
            if second is not None:
                raw_two = second + raw_two
        rest = zeroth - raw_two
    plus = 0.5 * (raw_two + raw_one)
    return plus - raw_one, rest, plus


def collide(f):
    g = [[[f[9 * a + 3 * b + c] for c in range(3)] for b in range(3)] for a in range(3)]
    even = [[g[2][b][c] + g[0][b][c] for c in range(3)] for b in range(3)]
    diff = [[g[2][b][c] - g[0][b][c] for c in range(3)] for b in range(3)]
    total = [[even[b][c] + g[1][b][c] for c in range(3)] for b in range(3)]
    t_even = [total[2][c] + total[0][c] for c in range(3)]
    t_diff = [total[2][c] - total[0][c] for c in range(3)]
    t_total = [t_even[c] + total[1][c] for c in range(3)]
    d_total = [diff[2][c] + diff[0][c] + diff[1][c] for c in range(3)]
    d_diff = [diff[2][c] - diff[0][c] for c in range(3)]
    e_total = [even[2][c] + even[0][c] + even[1][c] for c in range(3)]
    m002 = t_total[2] + t_total[0]
    jz = t_total[2] - t_total[0]
    rho = m002 + t_total[1]
    jy = t_diff[0] + t_diff[1] + t_diff[2]
    m011 = t_diff[2] - t_diff[0]
    m020 = t_even[0] + t_even[1] + t_even[2]
    jx = d_total[0] + d_total[1] + d_total[2]
    m101 = d_total[2] - d_total[0]
    m110 = d_diff[0] + d_diff[1] + d_diff[2]
    m200 = e_total[0] + e_total[1] + e_total[2]
    r = 1.0 / rho
    ux = (jx + 0.5 * body_force) * r
    uy = jy * r
    uz = jz * r
    s100 = ux * rho - jx
    s010 = uy * rho - jy
    s001 = uz * rho - jz
    k200 = m200 - ux * (jx - s100)
    k020 = m020 - uy * (jy - s010)
    k002 = m002 - uz * (jz - s001)
    k110 = m110 - ux * jy + uy * s100
    k101 = m101 - ux * jz + uz * s100
    k011 = m011 - uy * jz + uz * s010
    base = third * rho - (keep * third) * (k200 + k020 + k002)
    s200 = keep * k200 + base
    s020 = keep * k020 + base
    s002 = keep * k002 + base
    s110 = keep * k110
    s101 = keep * k101
    s011 = keep * k011
    d110 = 2.0 * s110
    d101 = 2.0 * s101
    d011 = 2.0 * s011
    q110 = d110 * s110
    q101 = d101 * s101
    q011 = d011 * s011
    p220 = s200 * s020 + q110
    s220 = p220 * r
    s202 = (s200 * s002 + q101) * r
    s022 = (s020 * s002 + q011) * r
    s211 = (s200 * s011 + d110 * s101) * r
    s121 = (s020 * s101 + d110 * s011) * r
    s112 = (s002 * s110 + d101 * s011) * r
    s222 = (p220 * s002 + q101 * s020 + q011 * s200 + 2.0 * d110 * s101 * d011) * (r * r)
    along_z = [[None] * 3 for _ in range(3)]
    along_z[0][0] = inverse_triple(rho, s001, s002, uz)
    along_z[1][0] = inverse_triple(s100, s101, None, uz)
    along_z[0][1] = inverse_triple(s010, s011, None, uz)
    along_z[2][0] = inverse_triple(s200, None, s202, uz)
    along_z[0][2] = inverse_triple(s020, None, s022, uz)
    along_z[1][1] = inverse_triple(s110, None, s112, uz)
    along_z[2][1] = inverse_triple(None, s211, None, uz)
    along_z[1][2] = inverse_triple(None, s121, None, uz)
    along_z[2][2] = inverse_triple(s220, None, s222, uz)
    out = [None] * 27
    for c in range(3):
        along_y = [
            inverse_triple(along_z[a][0][c], along_z[a][1][c], along_z[a][2][c], uy)
            for a in range(3)
        ]
        for b in range(3):
            triple = inverse_triple(along_y[0][b], along_y[1][b], along_y[2][b], ux)
            for a in range(3):
                out[9 * a + 3 * b + c] = triple[a]
    return out


def turn(value, shift):
    return pltpu.roll(value, shift % 128, axis=1) if shift % 128 else value


def number(cx, cy, cz):
    return 9 * (cx + 1) + 3 * (cy + 1) + cz + 1


def kernel(count_x, count_y, f_hbm, m_hbm, out, f, mask, post, rim, fringe, fringe_mask,
           y_out, y_in, d_in, e_out, e_in,
           ready, in_sem, x_send, x_recv, e_send, e_recv, y_send, y_recv):
    gx, gy = lax.axis_index("gx"), lax.axis_index("gy")
    depth = post.shape[3] - 2 * PAD
    tiles = depth // 8
    half = depth // 2

    def device(dx, dy):
        return (lax.rem(gx + dx + count_x, count_x), lax.rem(gy + dy + count_y, count_y))

    barrier = pltpu.get_barrier_semaphore()
    odd = lax.rem(gy, 2)

    def tell(semaphore, places):
        for dx, dy in places:
            pl.semaphore_signal(semaphore, inc=1, device_id=device(dx, dy), device_id_type=MESH)

    tell(barrier, ALONG_X)

    @pl.when(odd == 0)
    def _():
        tell(barrier, ACROSS)

    def load(j):
        rows = pl.ds(pl.multiple_of(8 * j, 8), 8)
        return pltpu.make_async_copy(f_hbm.at[:, :, rows], f.at[:, :, rows], in_sem.at[j])

    load_mask = pltpu.make_async_copy(m_hbm, mask.at[:, pl.ds(0, depth)], in_sem.at[tiles])
    load_mask.start()
    for j in range(tiles):
        load(j).start()

    lane = lax.broadcasted_iota(jnp.int32, (8, 128), 1)
    line = lax.broadcasted_iota(jnp.int32, (8, 128), 0)
    column = lane % 16
    plane = (lane // 16) % 4

    def among(lanes, planes):
        low, high = lanes
        here = (column >= low) & (column <= high) if low < high else column == low
        one = plane == planes[0]
        for other in planes[1:]:
            one = one | (plane == other)
        return here & one

    def x_copy(s, up, j):
        rows = pl.ds(PAD + half * j, half)
        lo = 18 if up else 0
        here, there = (2, 0) if up else (1, 3)
        return pltpu.make_async_remote_copy(
            src_ref=post.at[s, pl.ds(lo, NINE), here, rows],
            dst_ref=post.at[s, pl.ds(lo, NINE), there, rows],
            send_sem=x_send.at[s, up, j],
            recv_sem=x_recv.at[s, up, j],
            device_id=device(1 if up else -1, 0),
            device_id_type=MESH,
        )

    def e_copy(s, up):
        return pltpu.make_async_remote_copy(
            src_ref=e_out.at[s, up],
            dst_ref=e_in.at[s, up],
            send_sem=e_send.at[s, up],
            recv_sem=e_recv.at[s, up],
            device_id=device(1 if up else -1, 0),
            device_id_type=MESH,
        )

    def y_copy(up, dx):
        if dx:
            src, dst = y_out.at[up, (1 + dx) // 2], d_in.at[up, (1 - dx) // 2]
        else:
            src, dst = y_out.at[up], y_in.at[up]
        return pltpu.make_async_remote_copy(
            src_ref=src,
            dst_ref=dst,
            send_sem=y_send.at[up, dx + 1],
            recv_sem=y_recv.at[up, 1 - dx],
            device_id=device(dx, 1 if up else -1),
            device_id_type=MESH,
        )

    def shift_of(s):
        return 1 if s < STEPS - 1 else 1 - STEPS

    def streamed(s, p, cx, row):
        pops = {}
        for cz in (-1, 0, 1):
            for cy in (-1, 0, 1):
                value = post[s, number(cx, cy, cz), p + 1 - cx, pl.ds(PAD + row + shift_of(s) - cz, 8), :]
                if cy:
                    value = pltpu.roll(value, cy % 128, axis=1)
                pops[number(cx, cy, cz)] = value
        return pops

    def place_far(s, j):
        row = pl.multiple_of(8 * j, 8)
        for p in (0, 1):
            for index, value in streamed(s, p, 1 - 2 * p, row).items():
                f[index, p, pl.ds(row, 8), :] = value

    def relax(s, to):
        ahead = 0 if s else 0
        behind = 1 if s == STEPS - 1 else 2

        def body(j, carry):
            row = pl.multiple_of(8 * j, 8)
            again = jnp.where(j == 0, PAD + depth, jnp.where(j == tiles - 1, 0, PAD + row))
            again = pl.multiple_of(again, 8)
            if s:

                @pl.when(j == tiles // 2 - 1)
                def _():
                    for up in (0, 1):
                        x_copy(s - 1, up, 1).wait_recv()

            far = [streamed(s - 1, p, 1 - 2 * p, row) if s and not ahead else {} for p in (0, 1)]
            before = [
                [far[p][i] if i in far[p] else f[i, p, pl.ds(row, 8), :] for i in range(27)]
                for p in (0, 1)
            ]
            if ahead:
                place_far(s - 1, jnp.minimum(j + 1, tiles - 1))
            place_own(s, to, jnp.maximum(j - behind, 2 - behind))
            for p in (0, 1):
                pops = before[p]
                fluid = mask[p, pl.ds(row + s, 8), :] == 1
                after = collide(pops)
                for index in range(27):
                    value = jnp.where(fluid, after[index], pops[26 - index])
                    post[s, index, p + 1, pl.ds(PAD + row, 8), :] = value
                    post[s, index, p + 1, pl.ds(again, 8), :] = value
            if s:

                @pl.when(j % (tiles // 2) == tiles // 2 - 1)
                def _():
                    for up in (0, 1):
                        x_copy(s, up, j // (tiles // 2)).start()

            return carry

        if s:
            for up in (0, 1):
                x_copy(s - 1, up, 0).wait_recv()
            wrap_faces(s - 1, PAD, PAD + depth)
            if ahead:
                place_far(s - 1, 0)
        lax.fori_loop(0, tiles, body, 0)

    def finish_own(s, to):
        def body(k, carry):
            j = lax.rem(tiles - 1 + k, tiles) if s == STEPS - 1 else tiles - 2 + k
            place_own(s, to, j)
            return carry

        lax.fori_loop(0, 2, body, 0)

    def wrap_faces(s, start, end):
        for there, lo in ((0, 18), (3, 0)):
            for index in range(lo, lo + NINE):
                post[s, index, there, end : end + 8, :] = post[s, index, there, start : start + 8, :]

    def make_rim():
        def gather(index, tile):
            for v in (0, 1):
                packed = None
                for low in (0, 1):
                    for p in (0, 1):
                        start = 64 * low + 16 * (p + 1)
                        value = turn(tile(2 * v + low, p), start - 122)
                        here = (lane >= start) & (lane < start + 16)
                        packed = value if packed is None else jnp.where(here, value, packed)
                rim[index, v] = packed

        def body(third, carry):
            for k in range(3):
                index = 3 * third + k
                gather(index, lambda j, p: f[index, p, 8 * j : 8 * j + 8, :])
            return carry

        lax.fori_loop(0, NINE, body, 0)
        gather(MASK, lambda j, p: mask[p, 8 * j : 8 * j + 8, :].astype(jnp.float32))
        for v in (0, 1):
            pops = [rim[index, v] for index in range(27)]
            after = collide(pops)
            fluid = rim[MASK, v] == 1.0
            for index in range(27):
                rim[index, v] = jnp.where(fluid, after[index], pops[26 - index])

    def own_part(index, cy, v):
        value = None
        for shift, lanes in OWN[cy]:
            moved = turn(rim[index, v], shift)
            value = moved if value is None else jnp.where(among(lanes, (1, 2)), moved, value)
        return value

    def make_messages():
        for up in (0, 1):
            packed = [[jnp.zeros((8, 128), jnp.float32)] * 2 for _ in range(3)]
            for what, (pair, quarter) in SLOTS.items():
                right, around = quarter % 2, quarter // 2
                for cy in (-1, 0, 1):
                    if what is None and cy:
                        continue
                    index = number(what[0], cy, what[1]) if what else MASK
                    shift, (low, high), _, _ = SENT[up][cy]
                    here = among((low + 8 * right, high + 8 * right), (3, 0) if around else (1, 2))
                    for v in (0, 1):
                        value = turn(rim[index, v], shift + 8 * right + 32 * around)
                        packed[pair][v] = jnp.where(here, value, packed[pair][v])
            for pair in range(3):
                for v in (0, 1):
                    y_out[up, pair, v] = packed[pair][v]

    def from_side(tile, what, cy, up, across, planes, value):
        quarter = SLOTS[what][1]
        _, _, shift, lanes = SENT[up][cy]
        moved = turn(tile, shift - 8 * (quarter % 2) - 32 * (quarter // 2) + across)
        return jnp.where(among(lanes, planes), moved, value)

    def part_of(tile):
        if tile == 4:
            return [(NINE - 1, v, v) for v in (0, 1)]
        return [(4 * (tile // 2) + k, tile % 2, k) for k in range(4)]

    def send_fringe(s):
        for up in (0, 1):
            for tile in range(5):
                packed = None
                for q, v, quarter in part_of(tile):
                    value = turn(fringe[18 * up + q, v], 16 * (quarter - 1 - up))
                    packed = value if packed is None else jnp.where(plane == quarter, value, packed)
                e_out[s, up, tile] = packed
            e_copy(s, up).start()

    def receive_fringe(s):
        for up in (0, 1):
            e_copy(s, up).wait_recv()
            there = 0 if up else 3
            for tile in range(5):
                for q, v, quarter in part_of(tile):
                    index = 18 * up + q
                    moved = turn(e_in[s, up, tile], 16 * (there - quarter))
                    fringe[index, v] = jnp.where(plane == there, moved, fringe[index, v])

    def receive_sides():
        for up in (0, 1):
            for dx in (-1, 0, 1):
                y_copy(up, dx).wait_recv()
        for v in (0, 1):
            for what, (pair, _) in SLOTS.items():
                if what is None:
                    value = own_part(MASK, 0, v)
                    for up in (0, 1):
                        value = from_side(y_in[up, pair, v], what, 0, up, 0, (1, 2), value)
                    fringe_mask[v] = value
                    continue
                cx, cz = what
                for cy in (-1, 0, 1):
                    value = fringe[number(cx, cy, cz), v]
                    for up in (0, 1):
                        value = from_side(y_in[up, pair, v], what, cy, up, 0, (1, 2), value)
                        if cx:
                            near, there = (0, 0) if cx > 0 else (1, 3)
                            value = from_side(d_in[up, near, v], what, cy, up, -32 * cx, (there,), value)
                    fringe[number(cx, cy, cz), v] = value

    def moved_fringe(index):
        cx, cz = index // 9 - 1, index % 3 - 1
        pair = [turn(fringe[index, v], 16 * cx) for v in (0, 1)]
        if cz == 0:
            return pair
        pair = [pltpu.roll(value, cz % 8, axis=0) for value in pair]
        other = [turn(value, 64) for value in pair]
        first, second = (other[::-1], other) if cz > 0 else (other, other[::-1])
        edge = line == (0 if cz > 0 else 7)
        return [
            jnp.where(edge, jnp.where(lane < 64, first[v], second[v]), pair[v]) for v in (0, 1)
        ]

    def step_fringe():
        pops = [moved_fringe(index) for index in range(27)]
        for v in (0, 1):
            before = [pair[v] for pair in pops]
            after = collide(before)
            fluid = fringe_mask[v] == 1.0
            for index in range(27):
                value = jnp.where(fluid, after[index], before[26 - index])
                fringe[index, v] = turn(value, index // 3 % 3 - 1)

    def place_fringe(far):
        for index in range(27):
            cx = index // 9 - 1
            planes = [p for p in (0, 1) if (cx == 1 - 2 * p) == far]
            if not planes:
                continue
            pair = moved_fringe(index)
            for j in range(tiles):
                for p in planes:
                    start = 64 * (j % 2) + 16 * (p + 1)
                    left = turn(pair[j // 2], -start - 2)
                    right = turn(pair[j // 2], 125 - start - 10)
                    value = out[index, p, 8 * j : 8 * j + 8, :]
                    value = jnp.where(lane < 3, left, jnp.where(lane >= 125, right, value))
                    out[index, p, 8 * j : 8 * j + 8, :] = value

    def place_own(s, to, j):
        row = pl.multiple_of(8 * j, 8)
        for p in (0, 1):
            for cx in (0, 2 * p - 1):
                for cy in (-1, 0, 1):
                    for cz in (-1, 0, 1):
                        index = number(cx, cy, cz)
                        start = PAD + row + shift_of(s) - cz
                        value = post[s, index, p + 1 - cx, pl.ds(start, 8), :]
                        if cy:
                            value = pltpu.roll(value, cy % 128, axis=1)
                        to[index, p, pl.ds(row, 8), :] = value

    def place_faces(s, to):
        for up in (0, 1):
            x_copy(s, up, 0).wait_recv()
        for j in range(1, tiles + 1):
            if j == tiles // 2:
                for up in (0, 1):
                    x_copy(s, up, 1).wait_recv()
            if j == tiles:
                wrap_faces(s, depth, 0)
            row = 8 * (j % tiles)
            for p in (0, 1):
                for index, value in streamed(s, p, 1 - 2 * p, row).items():
                    to[index, p, row : row + 8, :] = value

    load_mask.wait()
    mask[:, depth : depth + 8, :] = mask[:, 0:8, :]
    for j in range(tiles):
        load(j).wait()
    make_rim()

    pl.when(odd == 1)(make_messages)

    def send_sides():
        for up in (0, 1):
            for dx in (0, -1, 1):
                y_copy(up, dx).start()

    @pl.when(odd == 1)
    def _():
        pl.semaphore_wait(barrier, len(ALONG_X) + len(ACROSS))
        tell(ready, ACROSS)
        send_sides()

    relax(0, f)

    @pl.when(odd == 0)
    def _():
        pl.semaphore_wait(barrier, len(ALONG_X))

    for j in (0, 1):
        for up in (0, 1):
            x_copy(0, up, j).start()
    for index in range(27):
        for v in (0, 1):
            fringe[index, v] = own_part(index, index // 3 % 3 - 1, v)
    send_fringe(0)
    pl.when(odd == 0)(make_messages)
    finish_own(0, f)
    relax(1, f)
    @pl.when(odd == 0)
    def _():
        pl.semaphore_wait(ready, len(ACROSS))
        send_sides()

    finish_own(1, f)

    receive_fringe(0)
    receive_sides()
    step_fringe()
    send_fringe(1)
    relax(2, out)
    receive_fringe(1)
    step_fringe()
    send_fringe(2)
    finish_own(2, out)
    place_fringe(False)
    for up in (0, 1):
        for dx in (-1, 0, 1):
            y_copy(up, dx).wait_send()
        for s in range(STEPS):
            e_copy(s, up).wait_send()
            for j in (0, 1):
                x_copy(s, up, j).wait_send()
    place_faces(2, out)
    receive_fringe(2)
    place_fringe(True)


def solution(mesh):
    count_x, count_y = mesh.shape["gx"], mesh.shape["gy"]

    def on_device(populations, fluid_mask):
        width_x, depth, width_y = fluid_mask.shape
        tall = depth + 2 * PAD

        def body(*refs):
            kernel(count_x, count_y, *refs)

        return pl.pallas_call(
            body,
            out_shape=pltpu.VMEM(populations.shape, jnp.float32),
            in_specs=[pl.BlockSpec(memory_space=pltpu.HBM)] * 2,
            out_specs=pl.BlockSpec(memory_space=pltpu.VMEM),
            scratch_shapes=[
                pltpu.VMEM(populations.shape, jnp.float32),
                pltpu.VMEM((width_x, depth + 8, width_y), jnp.int32),
                pltpu.VMEM((STEPS, 27, width_x + 2, tall, width_y), jnp.float32),
                pltpu.VMEM((MASK + 1, 2, 8, 128), jnp.float32),
                pltpu.VMEM((27, 2, 8, 128), jnp.float32),
                pltpu.VMEM((2, 8, 128), jnp.float32),
                pltpu.VMEM((2, 3, 2, 8, 128), jnp.float32),
                pltpu.VMEM((2, 3, 2, 8, 128), jnp.float32),
                pltpu.VMEM((2, 2, 2, 8, 128), jnp.float32),
                pltpu.VMEM((STEPS, 2, 5, 8, 128), jnp.float32),
                pltpu.VMEM((STEPS, 2, 5, 8, 128), jnp.float32),
                pltpu.SemaphoreType.REGULAR,
                pltpu.SemaphoreType.DMA((depth // 8 + 1,)),
                pltpu.SemaphoreType.DMA((STEPS, 2, 2)),
                pltpu.SemaphoreType.DMA((STEPS, 2, 2)),
                pltpu.SemaphoreType.DMA((STEPS, 2)),
                pltpu.SemaphoreType.DMA((STEPS, 2)),
                pltpu.SemaphoreType.DMA((2, 3)),
                pltpu.SemaphoreType.DMA((2, 3)),
            ],
            compiler_params=pltpu.CompilerParams(
                collective_id=0, has_side_effects=True, vmem_limit_bytes=60 * 2**20
            ),
            cost_estimate=pl.CostEstimate(
                flops=500 * STEPS * fluid_mask.size,
                bytes_accessed=8 * populations.size,
                transcendentals=0,
            ),
            name="lattice_steps",
        )(populations, fluid_mask)

    in_specs = (P(None, "gx", None, "gy"), P("gx", None, "gy"))
    out_specs = P(None, "gx", None, "gy")
    return jax.shard_map(
        on_device, mesh=mesh, in_specs=in_specs, out_specs=out_specs, check_vma=False
    )
```
